32 devices in a mesh: refl: 2 (over y), slab: 16 (over z, x, core).
Axes of the slice: x: 2, y: 2, z: 4, core: 2. Of those that a mesh axis runs over, the one named last changes fastest.
Arguments:
- amplitude: float32 [128, 128, 128], P('slab', 'refl'), may hold values from 1 to 3
- displacement: float32 [3, 128, 128, 128], P(None, 'slab', 'refl'), may hold values from -12 to 12
- support: int32 [128, 128, 128], P('slab'), may hold values from 0 to 1, as said below
- miller: int32 [2, 3], P('refl'), may hold values from -2 to 2, as said below
- shift_kz: int32 [2], P('refl'), may hold values from 0 to 255
- intensity: float32 [2, 256, 256, 256], P('refl', None, 'slab'), may hold values from 0.02 to 0.5
Outputs:
- grad_amplitude: float32 [128, 128, 128], P('slab', 'refl')
- grad_displacement: float32 [3, 128, 128, 128], P(None, 'slab', 'refl')
The draws below stay inside these ranges and needn't reach their ends.
Inputs may be any that keep to these rules, and one draw needn't show every extreme that they name: 1 inside the object's support, 0 outside. `miller`: no index is zero.
All inputs are finite; a program needn't handle non-finite values.
Results may differ from the reference program's by a relative error of at most 0.0003.
Values sent between devices are 32-bit elements; how exact they have to be, the bound alone decides.
No kernel may reach another device: no remote copies, remote signals or barrier semaphores. Data moves between devices by JAX's collectives and lax.ppermute only.
A program may use at most 64 MiB of HBM per device.

```python
import math
import jax
import jax.numpy as jnp
from jax import lax

SUP = 128
GRID = 256
REFLS = 2


def draw_support(key, part):
    keys = jax.random.split(jax.random.fold_in(key, 11), 2)
    offset = jnp.arange(SUP, dtype=jnp.int32) - SUP // 2
    square = offset * offset
    factors = jax.random.randint(keys[0], (3,), 3, 6)
    value = factors[0] * square[:, None, None] + factors[1] * square[None, :, None] + factors[2] * square[None, None, :]
    limit = 3 * (SUP // 2) * (SUP // 2)
    spread = SUP // 2 * (SUP // 2) // 2
    noise = jax.random.randint(keys[1], (SUP, SUP, SUP), -spread, spread)
    return jnp.where(value + noise < limit, 1, 0).astype(jnp.int32)


def draw_miller(key, part):
    keys = jax.random.split(jax.random.fold_in(key, 23), 2)
    magnitude = jax.random.randint(keys[0], (REFLS, 3), 1, 3)
    polarity = 2 * jax.random.randint(keys[1], (REFLS, 3), 0, 2) - 1
    drawn = (magnitude * polarity).astype(jnp.int32)
    drawn = drawn.at[0, 0].set(2)
    drawn = drawn.at[0, 1].set(-2)
    return drawn.astype(jnp.int32)


def shard_levels(key, dims, cuts, least, high):
    level = 1.0
    for axis_at, shards_of in cuts:
        draws = jax.random.uniform(jax.random.fold_in(jax.random.fold_in(key, 6), axis_at), (shards_of,), jnp.float32, least / len(cuts), high / len(cuts))
        level = level * jnp.repeat(jnp.exp(draws), dims[axis_at] // shards_of).reshape((-1,) + (1,) * (len(dims) - 1 - axis_at))
    return level


def scatter_about(own_key, shape, width, bound, shards=(), kind=jnp.bfloat16):
    result = jax.random.normal(own_key, shape, jnp.float32) * width
    if len(shards) > 0:
        result = shard_levels(own_key, shape, shards, -0.22, 0.18) * result
    return jnp.clip(result, min=-bound, max=bound).astype(kind)


def setup_inputs(seed: int = 0) -> dict:
    key_of = jax.random.split(jax.random.key(seed), 7)
    amplitude = jnp.clip(1.0 + 2.0 * jax.random.uniform(key_of[0], (SUP, SUP, SUP), jnp.float32) ** shard_levels(key_of[0], (SUP, SUP, SUP), ((0, 16), (1, 2)), -0.2, 0.2), 1.0, 3.0)
    displacement = scatter_about(key_of[1], (3, SUP, SUP, SUP), 2.0, 12.0, ((1, 16), (2, 2)), jnp.float32)
    support = draw_support(jax.random.fold_in(key_of[6], 71), 0)
    miller = draw_miller(jax.random.fold_in(key_of[6], 71), 0)
    shift_kz = jax.random.randint(key_of[4], (REFLS,), 0, GRID).astype(jnp.int32)
    intensity = jnp.clip(jnp.exp(math.log(0.5) - 3.218876 * jax.random.uniform(key_of[5], (REFLS, GRID, GRID, GRID), jnp.float32) ** shard_levels(key_of[5], (REFLS, GRID, GRID, GRID), ((0, 2), (2, 16)), -0.2, 0.2)), 0.02, 0.5)
    return {"amplitude": amplitude, "displacement": displacement, "support": support, "miller": miller, "shift_kz": shift_kz, "intensity": intensity}


STRAIN_WEIGHT = 0.05
EDGE_WEIGHT = 0.05


def laplace(field):
    padded = jnp.pad(field, 1)
    beside = padded[2:, 1:-1, 1:-1] + padded[:-2, 1:-1, 1:-1]
    beside = beside + padded[1:-1, 2:, 1:-1] + padded[1:-1, :-2, 1:-1]
    beside = beside + padded[1:-1, 1:-1, 2:] + padded[1:-1, 1:-1, :-2]
    return 6.0 * field - beside


def reference(amplitude, displacement, support, miller, shift_kz, intensity):
    mask = support.astype(amplitude.dtype)
    weight = mask * amplitude

    def one_reflection(carry, index):
        row = miller[index].astype(amplitude.dtype)
        phase = row[0] * displacement[0] + row[1] * displacement[1] + row[2] * displacement[2]
        cosine = jnp.cos(phase)
        sine = jnp.sin(phase)
        target = weight * cosine + 1j * (weight * sine)
        padded = jnp.zeros((GRID, GRID, GRID), target.dtype).at[:SUP, :SUP, :SUP].set(target)
        spectrum = jnp.fft.fftn(padded, norm="ortho")
        measured = jnp.roll(intensity[index], -shift_kz[index], axis=2)
        power = jnp.real(spectrum) ** 2 + jnp.imag(spectrum) ** 2
        residual = 4.0 * (power - measured) * spectrum
        back = jnp.fft.ifftn(residual, norm="ortho")[:SUP, :SUP, :SUP]
        along = jnp.real(back) * cosine + jnp.imag(back) * sine
        across = weight * (jnp.imag(back) * cosine - jnp.real(back) * sine)
        grad_amp = carry[0] + mask * along
        grad_disp = carry[1] + row[:, None, None, None] * across[None]
        return (grad_amp, grad_disp), None

    start = (jnp.zeros_like(amplitude), jnp.zeros_like(displacement))
    (grad_amp, grad_disp), unused = lax.scan(one_reflection, start, jnp.arange(REFLS, dtype=jnp.int32))
    grad_amp = grad_amp + 2.0 * EDGE_WEIGHT * mask * laplace(weight)
    strain = jnp.stack([laplace(displacement[comp]) for comp in range(3)])
    grad_disp = grad_disp + 2.0 * STRAIN_WEIGHT * strain
    return grad_amp, grad_disp
```

```python
import functools

import jax
import jax.numpy as jnp
import ml_dtypes
import numpy as np
from jax import lax
from jax.experimental import pallas as pl
from jax.experimental.pallas import tpu as pltpu
from jax.sharding import PartitionSpec as P

STRAIN_WEIGHT = 0.05
EDGE_WEIGHT = 0.05
F32 = jnp.float32
BF16 = jnp.bfloat16


def split_table(table):
    high = table.astype(ml_dtypes.bfloat16)
    low = (table - high.astype(np.float64)).astype(ml_dtypes.bfloat16)
    return high, low


def forward_table(freqs, places, length):
    angle = 2.0 * np.pi / length * (freqs[:, None] * places[None, :] % length)
    cosine = np.cos(angle) * length ** (-0.5)
    sine = np.sin(angle) * length ** (-0.5)
    return np.block([[cosine, sine], [-sine, cosine]])


def turn_fits():
    nodes = np.cos(np.pi * (np.arange(400) + 0.5) / 400)
    t = (nodes + 1.0) / 8.0
    r = np.sqrt(t)
    fits = []
    for values, degree in ((np.cos(2 * np.pi * r), 8), (np.sin(2 * np.pi * r) / r, 8)):
        cheb = np.polynomial.chebyshev.Chebyshev.fit(t, values, degree, domain=[0.0, 0.25])
        fits.append([float(c) for c in cheb.convert(kind=np.polynomial.Polynomial).coef])
    return fits


COS_FIT, SIN_FIT = turn_fits()


def series(coefs, t):
    total = jnp.full_like(t, coefs[-1])
    for coef in coefs[-2::-1]:
        total = total * t + coef
    return total


def halves(x):
    high = x.astype(BF16)
    return high, (x - high.astype(F32)).astype(BF16)


def dot(a, b):
    return jnp.dot(a, b, preferred_element_type=F32)


def dot_pairs(a, b):
    return dot(a[0], b[0]) + (dot(a[0], b[1]) + dot(a[1], b[0]))


def vmem(count):
    return [pl.BlockSpec(memory_space=pltpu.VMEM)] * count


SMEM = pl.BlockSpec(memory_space=pltpu.SMEM)


def call(kernel, outs, in_specs, scratch, flops, moved, name, grid=()):
    return pl.pallas_call(
        kernel,
        grid=grid,
        out_shape=[jax.ShapeDtypeStruct(s, F32) for s in outs],
        in_specs=in_specs,
        out_specs=vmem(len(outs)),
        scratch_shapes=scratch,
        compiler_params=pltpu.CompilerParams(vmem_limit_bytes=48 * 1024 * 1024),
        cost_estimate=pl.CostEstimate(flops=flops, bytes_accessed=moved, transcendentals=0),
        name=name,
    )


def object_kernel(refls, grid, place, params, amp, disp, sup, *outs):
    planes, rows, depth = amp.shape
    first = pl.multiple_of(place[2] * rows, rows)
    zed = lax.broadcasted_iota(jnp.int32, (rows, depth), 1).astype(F32) * (1.0 / grid)

    def plane(p, carry):
        weight = sup[p, pl.ds(first, rows), :].astype(F32) * amp[p]
        parts = [disp[0, p], disp[1, p], disp[2, p]]
        for k in range(refls):
            phase = params[4 * k] * parts[0] + params[4 * k + 1] * parts[1] + params[4 * k + 2] * parts[2]
            shifted = params[4 * k + 3] * zed
            turns = phase * (0.5 / np.pi) + (shifted - jnp.floor(shifted))
            turns = turns - jnp.floor(turns + 0.5)
            square = turns * turns
            cosine = series(COS_FIT, square)
            sine = series(SIN_FIT, square) * turns
            outs[k][0, p] = weight * cosine
            outs[k][1, p] = weight * sine
            outs[refls + k][0, p] = cosine
            outs[refls + k][1, p] = sine
        return carry

    lax.fori_loop(0, planes, plane, 0)


def y_forward_kernel(refls, chips, place, *refs):
    parts, (high, low), outs = refs[: 2 * refls], refs[2 * refls : 2 * refls + 2], refs[2 * refls + 2 : -2]
    hold_high, hold_low = refs[-2:]
    chip, core, refl = place[0], place[1], place[2]
    planes, rows, depth = parts[0].shape[1:]
    length = rows * refls
    share = high.shape[1] // chips

    def order(table):
        return jnp.concatenate(
            [table[core, pl.ds(pl.multiple_of((chip ^ k) * share, share), share), :] for k in range(chips)], axis=0
        )

    table = (order(high), order(low))
    for src in range(2):
        for p in range(planes):
            lane = (src * planes + p) * depth
            for c in range(2):
                for k in range(refls):
                    one, two = halves(parts[src * refls + k][c, p])
                    at = pl.ds(pl.multiple_of(c * length + (refl ^ k) * rows, rows), rows)
                    hold_high[at, lane : lane + depth] = one
                    hold_low[at, lane : lane + depth] = two
    for src in range(2):
        for p in range(0, planes, 2):
            lane = (src * planes + p) * depth
            operand = (hold_high[:, lane : lane + 2 * depth], hold_low[:, lane : lane + 2 * depth])
            result = dot_pairs(table, operand)
            base = (core if src == 0 else 1 - core) * planes + p
            for k in range(chips):
                for j in range(2):
                    outs[k][base + j] = result[k * share : (k + 1) * share, j * depth : (j + 1) * depth]


def middle_kernel(chips, place, *refs):
    got, intensity = refs[:chips], refs[chips]
    fwd_high, fwd_low, bwd_high, bwd_low = refs[chips + 1 : chips + 5]
    outs = refs[chips + 5 : 2 * chips + 5]
    gather, scatter = refs[2 * chips + 5 :]
    chip = place[0]
    group, width, depth = got[0].shape
    rows = width // 2
    edge = group * chips
    grid = 2 * edge
    for pair in range(0, rows, 2):
        for k in range(chips):
            for c in range(2):
                at = pl.ds(pl.multiple_of(c * edge + (chip ^ k) * group, group), group)
                for j in range(2):
                    gather[at, j * depth : (j + 1) * depth] = got[k][:, c * rows + pair + j, :]
        forward = (fwd_high[...], fwd_low[...])
        adjoint = (bwd_high[...], bwd_low[...])
        one = dot_pairs(forward, halves(gather[...]))
        lines = jnp.concatenate(
            [
                jnp.concatenate([one[:grid, j * depth : (j + 1) * depth], one[grid:, j * depth : (j + 1) * depth]], axis=1)
                for j in range(2)
            ],
            axis=0,
        )
        spectrum = dot_pairs(halves(lines), adjoint)
        real, imag = spectrum[:, :grid], spectrum[:, grid:]
        measured = jnp.concatenate([intensity[0, :, pair, :], intensity[0, :, pair + 1, :]], axis=0)
        excess = 4.0 * (real * real + imag * imag - measured)
        residual = jnp.concatenate([excess * real, excess * imag], axis=1)
        back = dot_pairs(halves(residual), forward)
        lines = jnp.concatenate(
            [
                jnp.concatenate([back[:grid, c * depth : (c + 1) * depth], back[grid:, c * depth : (c + 1) * depth]], axis=1)
                for c in range(2)
            ],
            axis=0,
        )
        scatter[...] = dot_pairs(adjoint, halves(lines))
        for k in range(chips):
            for c in range(2):
                at = pl.ds(pl.multiple_of(c * edge + (chip ^ k) * group, group), group)
                for j in range(2):
                    outs[k][:, c * rows + pair + j, :] = scatter[at, j * depth : (j + 1) * depth]


def y_adjoint_kernel(refls, chips, chunks, mate, place, *refs):
    got, (high, low), outs = refs[: chunks * chips], refs[chunks * chips : chunks * chips + 2], refs[chunks * chips + 2 : -1]
    hold = refs[-1]
    chip, core, refl = place[0], place[1], place[2]
    parts, planes, rows, depth = outs[0].shape
    length = rows * refls
    width = got[0].shape[1]
    table = (high[core], low[core])
    base = (1 - core if mate else core) * planes
    for p in range(0, planes, 2):
        for q in range(chunks):
            for k in range(chips):
                at = pl.ds(pl.multiple_of((q * chips + (chip ^ k)) * width, width), width)
                for j in range(2):
                    hold[at, (p + j) * depth : (p + j + 1) * depth] = got[q * chips + k][base + p + j]
    for p in range(0, planes, 2):
        result = dot_pairs(table, halves(hold[:, p * depth : (p + 2) * depth]))
        for q in range(refls):
            for c in range(2):
                at = (q * 2 + c) * rows
                for j in range(2):
                    value = result[at : at + rows, j * depth : (j + 1) * depth]
                    for k in range(refls):

                        @pl.when((refl ^ k) == q)
                        def _():
                            outs[k][c, p + j] = value


def add_kernel(a, b, out):
    out[...] = a[...] + b[...]


def final_kernel(refls, place, params, *refs):
    amp, sup, lapped, own, mate = refs[:5]
    others = refs[5 : 5 + refls - 1]
    phases = refs[5 + refls - 1 : 5 + 2 * refls - 1]
    out_amp, out_disp = refs[-2:]
    planes, rows, depth = amp.shape
    first = pl.multiple_of(place[2] * rows, rows)

    def plane(p, carry):
        mask = sup[p, pl.ds(first, rows), :].astype(F32)
        weight = mask * amp[p]
        total = jnp.zeros((rows, depth), F32)
        moved = [jnp.zeros((rows, depth), F32) for _ in range(3)]
        for k in range(refls):
            if k == 0:
                real, imag = own[0, p] + mate[0, p], own[1, p] + mate[1, p]
            else:
                real, imag = others[k - 1][0, p], others[k - 1][1, p]
            cosine, sine = phases[k][0, p], phases[k][1, p]
            total = total + (real * cosine + imag * sine)
            across = weight * (imag * cosine - real * sine)
            moved = [m + params[4 * k + c] * across for c, m in enumerate(moved)]
        out_amp[p] = mask * total + (2.0 * EDGE_WEIGHT) * (mask * lapped[0, p])
        for c in range(3):
            out_disp[c, p] = moved[c] + (2.0 * STRAIN_WEIGHT) * lapped[c + 1, p]
        return carry

    lax.fori_loop(0, planes, plane, 0)


def with_halo(cells, sides, width):
    for axis, dim in sides:
        count = lax.axis_size(axis)
        ends = count - 1
        head = lax.slice_in_dim(cells, 0, width, axis=dim)
        tail = lax.slice_in_dim(cells, cells.shape[dim] - width, cells.shape[dim], axis=dim)
        cells = jnp.concatenate(
            [
                lax.ppermute(tail, axis, [(i, (i + 1) % count) for i in range(ends)]),
                cells,
                lax.ppermute(head, axis, [((i + 1) % count, i) for i in range(ends)]),
            ],
            axis=dim,
        )
    return cells


def regulariser(fields):
    extended = with_halo(fields, (("refl", 2), ("slab", 1)), 1)
    extended = jnp.pad(extended, ((0, 0), (0, 0), (0, 0), (1, 1)))
    centre = extended[:, 1:-1, 1:-1, 1:-1]
    beside = extended[:, 2:, 1:-1, 1:-1] + extended[:, :-2, 1:-1, 1:-1]
    beside = beside + extended[:, 1:-1, 2:, 1:-1] + extended[:, 1:-1, :-2, 1:-1]
    beside = beside + extended[:, 1:-1, 1:-1, 2:] + extended[:, 1:-1, 1:-1, :-2]
    return 6.0 * centre - beside


def swap(x, axis, bits):
    count = lax.axis_size(axis)
    return lax.ppermute(x, axis, [(i, i ^ bits) for i in range(count)])


def body(amplitude, displacement, support, miller, shift_kz, intensity):
    refls = lax.axis_size("refl")
    slabs = lax.axis_size("slab")
    chips = slabs // 2
    planes, rows, depth = amplitude.shape
    edge = planes * slabs
    grid = 2 * edge
    keys = grid // slabs
    chunk = 8
    chunks = keys // chunk
    refl = lax.axis_index("refl")
    slab = lax.axis_index("slab")
    place = jnp.stack([slab // 2, slab % 2, refl]).astype(jnp.int32)
    cells = planes * rows * depth

    every, inner = np.arange(grid), np.arange(edge)
    table = forward_table(every, inner, grid)
    fwd, bwd = split_table(table), split_table(table.T)
    y_fwd, y_bwd = [], []
    by_chunk = table.reshape(2, chips, 2, chunks, chunk, 2 * edge)
    for q in range(chunks):
        y_fwd.append(split_table(by_chunk[:, :, :, q].transpose(2, 1, 0, 3, 4).reshape(2, chips * 2 * chunk, 2 * edge)))
    back = by_chunk.transpose(2, 5, 3, 1, 0, 4).reshape(2, 2, refls, rows, chunks * chips * 2 * chunk)
    y_bwd = split_table(back.transpose(0, 2, 1, 3, 4).reshape(2, 2 * edge, chunks * chips * 2 * chunk))

    own_params = jnp.concatenate([miller[0].astype(F32), shift_kz.astype(F32)])
    params = jnp.concatenate([own_params] + [swap(own_params, "refl", k) for k in range(1, refls)])

    made = call(
        functools.partial(object_kernel, refls, grid),
        [(2, planes, rows, depth)] * (2 * refls),
        [SMEM, SMEM] + vmem(3),
        [],
        100 * refls * cells,
        cells * 4 * (5 + 4 * refls),
        "object",
    )(place, params, amplitude, displacement, support)
    parts, phases = made[:refls], made[refls:]
    held = [parts[0]] + [swap(parts[k], "refl", k) for k in range(1, refls)]
    mates = [swap(x, "slab", 1) for x in held]

    mask_own = lax.dynamic_slice_in_dim(support, refl * rows, rows, 1).astype(F32)
    fields = jnp.concatenate([(mask_own * amplitude)[None], displacement], axis=0)
    lapped = regulariser(fields)

    group = 2 * planes
    sent_shape = (group, 2 * chunk, depth)
    returned = []
    arrived = []
    for q in range(chunks):
        high, low = y_fwd[q]
        sends = call(
            functools.partial(y_forward_kernel, refls, chips),
            [sent_shape] * chips,
            [SMEM] + vmem(2 * refls + 2),
            [pltpu.VMEM((2 * edge, group * depth), BF16)] * 2,
            6 * group * depth * 2 * edge * high.shape[1],
            4 * group * depth * (2 * edge + high.shape[1]),
            "y_forward",
        )(place, *held, *mates, jnp.asarray(high), jnp.asarray(low))
        arrived.append([sends[0]] + [swap(sends[k], "slab", 2 * k) for k in range(1, chips)])
    for q in range(chunks):
        backs = call(
            functools.partial(middle_kernel, chips),
            [sent_shape] * chips,
            [SMEM]
            + vmem(chips)
            + [pl.BlockSpec((1, grid, chunk, grid), functools.partial(lambda at, step: (0, 0, at, 0), q))]
            + vmem(4),
            [pltpu.VMEM((2 * edge, 2 * depth), F32)] * 2,
            6 * chunk * (2 * edge * 2 * grid * depth * 2 + grid * 2 * depth * 2 * grid * 2),
            4 * (2 * chips * group * 2 * chunk * depth + grid * grid * chunk),
            "middle",
            (1,),
        )(place, *arrived[q], intensity, *[jnp.asarray(t) for t in fwd + bwd])
        returned.append([backs[0]] + [swap(backs[k], "slab", 2 * k) for k in range(1, chips)])

    flat = [x for chunk_of in returned for x in chunk_of]

    def y_adjoint(mate):
        return call(
            functools.partial(y_adjoint_kernel, refls, chips, chunks, mate),
            [(2, planes, rows, depth)] * refls,
            [SMEM] + vmem(chunks * chips + 2),
            [pltpu.VMEM((2 * edge, planes * depth), F32)],
            6 * planes * depth * 4 * edge * edge,
            4 * planes * depth * 4 * edge,
            "y_adjoint",
        )(place, *flat, jnp.asarray(y_bwd[0]), jnp.asarray(y_bwd[1]))

    for_mate = y_adjoint(True)
    from_mate = [swap(x, "slab", 1) for x in for_mate]
    mine = y_adjoint(False)
    others = []
    for k in range(1, refls):
        (whole,) = call(
            add_kernel, [(2, planes, rows, depth)], vmem(2), [], 2 * cells, 24 * cells, "add"
        )(mine[k], from_mate[k])
        others.append(swap(whole, "refl", k))

    return tuple(
        call(
            functools.partial(final_kernel, refls),
            [(planes, rows, depth), (3, planes, rows, depth)],
            [SMEM, SMEM] + vmem(5 + refls - 1 + refls),
            [],
            20 * refls * cells,
            4 * cells * (12 + 4 * refls),
            "final",
        )(place, params, amplitude, support, lapped, mine[0], from_mate[0], *others, *phases)
    )


def solution(mesh):
    placed = (
        P("slab", "refl", None),
        P(None, "slab", "refl", None),
        P("slab", None, None),
        P("refl", None),
        P("refl"),
        P("refl", None, "slab", None),
    )
    return jax.shard_map(
        body,
        mesh=mesh,
        in_specs=placed,
        out_specs=(P("slab", "refl", None), P(None, "slab", "refl", None)),
        check_vma=False,
    )
```

```python
import functools

import jax
import jax.numpy as jnp
import ml_dtypes
import numpy as np
from jax import lax
from jax.experimental import pallas as pl
from jax.experimental.pallas import tpu as pltpu
from jax.sharding import PartitionSpec as P

STRAIN_WEIGHT = 0.05
EDGE_WEIGHT = 0.05
PIECES = (8, 8)
ORDER = (4, 5, 6, 7, 1, 2, 3)
LATE = (1, 2, 3)
F32 = jnp.float32
BF16 = jnp.bfloat16


def split_table(table):
    high = table.astype(ml_dtypes.bfloat16)
    low = (table - high.astype(np.float64)).astype(ml_dtypes.bfloat16)
    return high, low


def forward_table(freqs, places, length):
    angle = 2.0 * np.pi / length * (freqs[:, None] * places[None, :] % length)
    cosine = np.cos(angle) * length ** (-0.5)
    sine = np.sin(angle) * length ** (-0.5)
    return np.block([[cosine, sine], [-sine, cosine]])


def turn_fits():
    nodes = np.cos(np.pi * (np.arange(400) + 0.5) / 400)
    t = (nodes + 1.0) / 8.0
    r = np.sqrt(t)
    fits = []
    for values, degree in ((np.cos(2 * np.pi * r), 8), (np.sin(2 * np.pi * r) / r, 8)):
        cheb = np.polynomial.chebyshev.Chebyshev.fit(t, values, degree, domain=[0.0, 0.25])
        fits.append([float(c) for c in cheb.convert(kind=np.polynomial.Polynomial).coef])
    return fits


COS_FIT, SIN_FIT = turn_fits()


def series(coefs, t):
    total = jnp.full_like(t, coefs[-1])
    for coef in coefs[-2::-1]:
        total = total * t + coef
    return total


def halves(x):
    high = x.astype(BF16)
    return high, (x - high.astype(F32)).astype(BF16)


def dot(a, b):
    return jnp.dot(a, b, preferred_element_type=F32)


def dot_pairs(a, b):
    return dot(a[0], b[0]) + (dot(a[0], b[1]) + dot(a[1], b[0]))


SMEM = pl.BlockSpec(memory_space=pltpu.SMEM)


def whole(shape):
    return pl.BlockSpec(tuple(shape), lambda step, rank=len(shape): (0,) * rank)


def call(kernel, outs, scalars, operands, scratch, flops, name, blocks=None):
    blocks = blocks or {}
    specs = [SMEM] * len(scalars)
    moved = 4 * sum(int(np.prod(shape)) for shape in outs)
    for at, operand in enumerate(operands):
        if at in blocks:
            shape, index = blocks[at]
            specs.append(pl.BlockSpec(shape, lambda step, index=index: index))
        else:
            shape = operand.shape
            specs.append(whole(shape))
        moved += int(np.prod(shape)) * operand.dtype.itemsize
    return pl.pallas_call(
        kernel,
        grid=(1,),
        out_shape=[jax.ShapeDtypeStruct(shape, F32) for shape in outs],
        in_specs=specs,
        out_specs=[whole(shape) for shape in outs],
        scratch_shapes=scratch,
        compiler_params=pltpu.CompilerParams(vmem_limit_bytes=48 * 1024 * 1024),
        cost_estimate=pl.CostEstimate(flops=int(flops), bytes_accessed=int(moved), transcendentals=0),
        name=name,
    )(*scalars, *operands)


def edges_kernel(place, amp, disp, sup, x_mate, x_out, y_first, y_last):
    planes, rows, depth = amp.shape
    first = pl.multiple_of(place[2] * rows, rows)
    core = place[1]

    def field(f, p):
        if f == 0:
            return sup[p, pl.ds(first, rows), :].astype(F32) * amp[p]
        return disp[f - 1, p]

    for f in range(4):
        x_mate[f] = field(f, (1 - core) * (planes - 1))
        x_out[f] = field(f, core * (planes - 1))
        for p in range(planes):
            value = field(f, p)
            y_first[f, p : p + 1, :] = value[:1]
            y_last[f, p : p + 1, :] = value[rows - 1 :]


def laplace_kernel(place, amp, disp, sup, x_mate, x_out, y_before, y_after, out):
    planes, rows, depth = amp.shape
    first = pl.multiple_of(place[2] * rows, rows)
    low_core = place[1] == 0
    row = lax.broadcasted_iota(jnp.int32, (rows, depth), 0)
    lane = lax.broadcasted_iota(jnp.int32, (rows, depth), 1)

    def field(f, p):
        if f == 0:
            return sup[p, pl.ds(first, rows), :].astype(F32) * amp[p]
        return disp[f - 1, p]

    for f in range(4):
        for p in range(planes):
            centre = field(f, p)
            beside = jnp.where(low_core, x_out[f], x_mate[f]) if p == 0 else field(f, p - 1)
            beside = beside + (jnp.where(low_core, x_mate[f], x_out[f]) if p == planes - 1 else field(f, p + 1))
            beside = beside + jnp.where(row == 0, y_before[f, p : p + 1, :], pltpu.roll(centre, 1, 0))
            beside = beside + jnp.where(row == rows - 1, y_after[f, p : p + 1, :], pltpu.roll(centre, rows - 1, 0))
            beside = beside + jnp.where(lane == 0, 0.0, pltpu.roll(centre, 1, 1))
            beside = beside + jnp.where(lane == depth - 1, 0.0, pltpu.roll(centre, depth - 1, 1))
            out[f, p] = 6.0 * centre - beside


def object_kernel(which, grid, place, params, amp, disp, sup, *outs):
    planes, rows, depth = amp.shape
    first = pl.multiple_of(place[2] * rows, rows)
    zed = lax.broadcasted_iota(jnp.int32, (rows, depth), 1).astype(F32) * (1.0 / grid)
    each = len(outs) // len(which)
    portion = planes // (each - 1)

    for part in range(each - 1):

        def plane(i, carry, part=part):
            p = part * portion + i
            weight = sup[p, pl.ds(first, rows), :].astype(F32) * amp[p]
            parts = [disp[0, p], disp[1, p], disp[2, p]]
            for at, k in enumerate(which):
                phase = params[4 * k] * parts[0] + params[4 * k + 1] * parts[1] + params[4 * k + 2] * parts[2]
                shifted = params[4 * k + 3] * zed
                turns = phase * (0.5 / np.pi) + (shifted - jnp.floor(shifted))
                turns = turns - jnp.floor(turns + 0.5)
                square = turns * turns
                cosine = series(COS_FIT, square)
                sine = series(SIN_FIT, square) * turns
                outs[each * at][0, p] = cosine
                outs[each * at][1, p] = sine
                outs[each * at + 1 + part][0, i] = weight * cosine
                outs[each * at + 1 + part][1, i] = weight * sine
            return carry

        lax.fori_loop(0, portion, plane, 0)


def y_forward_kernel(refls, chips, splits, place, *refs):
    count = 2 * refls * splits
    parts, (high, low), outs = refs[:count], refs[count : count + 2], refs[count + 2 : -2]
    hold_high, hold_low = refs[-2:]
    chip, core, refl = place[0], place[1], place[2]
    portion, rows, depth = parts[0].shape[1:]
    planes = portion * splits
    length = rows * refls
    share = high.shape[1] // chips

    def order(table):
        return jnp.concatenate(
            [table[core, pl.ds(pl.multiple_of((chip ^ k) * share, share), share), :] for k in range(chips)], axis=0
        )

    table = (order(high), order(low))
    for src in range(2):
        for p in range(planes):
            lane = (src * planes + p) * depth
            for c in range(2):
                for k in range(refls):
                    part = parts[(src * refls + k) * splits + p // portion]
                    one, two = halves(part[c, p % portion])
                    at = pl.ds(pl.multiple_of(c * length + (refl ^ k) * rows, rows), rows)
                    hold_high[at, lane : lane + depth] = one
                    hold_low[at, lane : lane + depth] = two
    for src in range(2):
        for p in range(0, planes, 2):
            lane = (src * planes + p) * depth
            operand = (hold_high[:, lane : lane + 2 * depth], hold_low[:, lane : lane + 2 * depth])
            result = dot_pairs(table, operand)
            base = (core if src == 0 else 1 - core) * planes + p
            for k in range(chips):
                for j in range(2):
                    outs[k][base + j] = result[k * share : (k + 1) * share, j * depth : (j + 1) * depth]


def middle_kernel(chips, skip, place, *refs):
    got, intensity = refs[:chips], refs[chips]
    fwd = (refs[chips + 1][...], refs[chips + 2][...])
    bwd = (refs[chips + 3][...], refs[chips + 4][...])
    outs = refs[chips + 5 : -2]
    gather, scatter = refs[-2:]
    chip = place[0]
    group, width, depth = got[0].shape
    rows = width // 2
    edge = group * chips
    grid = 2 * edge
    batch = gather.shape[1] // depth

    def place_of(c, k):
        return pl.ds(pl.multiple_of(c * edge + (chip ^ k) * group, group), group)

    for key in range(0, rows, batch):
        for k in range(chips):
            for c in range(2):
                for j in range(batch):
                    gather[place_of(c, k), j * depth : (j + 1) * depth] = got[k][:, (key + j) * 2 + c, :]
        one = dot_pairs(fwd, halves(gather[...]))
        lines = jnp.concatenate(
            [
                jnp.concatenate([one[c * grid : (c + 1) * grid, j * depth : (j + 1) * depth] for c in range(2)], axis=1)
                for j in range(batch)
            ],
            axis=0,
        )
        spectrum = dot_pairs(halves(lines), bwd)
        real, imag = spectrum[:, :grid], spectrum[:, grid:]
        measured = jnp.concatenate([intensity[0, :, skip + key + j, :] for j in range(batch)], axis=0)
        excess = 4.0 * (real * real + imag * imag - measured)
        residual = jnp.concatenate([excess * real, excess * imag], axis=1)
        back = dot_pairs(halves(residual), fwd)
        lines = jnp.concatenate(
            [
                jnp.concatenate([back[j * grid : (j + 1) * grid, c * depth : (c + 1) * depth] for j in range(batch)], axis=1)
                for c in range(2)
            ],
            axis=0,
        )
        scatter[...] = dot_pairs(bwd, halves(lines))
        for k in range(chips):
            for c in range(2):
                for j in range(batch):
                    outs[k][:, (key + j) * 2 + c, :] = scatter[place_of(c, k), j * depth : (j + 1) * depth]


def y_adjoint_kernel(refls, chips, jobs, place, *refs):
    got, (high, low) = refs[:chips], refs[chips : chips + 2]
    total = refls * len(jobs)
    adds, outs = refs[chips + 2 : -1 - total], refs[-1 - total : -1]
    hold = refs[-1]
    chip, core, refl = place[0], place[1], place[2]
    planes, rows, depth = outs[0].shape[1:]
    width = got[0].shape[1]

    def order(table):
        pieces = []
        for q in range(refls):
            for c in range(2):
                at = pl.multiple_of(((refl ^ q) * 2 + c) * rows, rows)
                pieces.append(table[core, pl.ds(at, rows), :])
        return jnp.concatenate(pieces, axis=0)

    table = (order(high), order(low))
    for job, (mate, first) in enumerate(jobs):
        base = (1 - core if mate else core) * (got[0].shape[0] // 2) + first
        for p in range(planes):
            lane = (job * planes + p) * depth
            for k in range(chips):
                at = pl.ds(pl.multiple_of((chip ^ k) * width, width), width)
                hold[at, lane : lane + depth] = got[k][base + p]
    for job in range(len(jobs)):
        for p in range(0, planes, 2):
            lane = (job * planes + p) * depth
            result = dot_pairs(table, halves(hold[:, lane : lane + 2 * depth]))
            for k in range(refls):
                for c in range(2):
                    at = (k * 2 + c) * rows
                    for j in range(2):
                        value = result[at : at + rows, j * depth : (j + 1) * depth]
                        if adds:
                            value = value + adds[job * refls + k][c, p + j]
                        outs[job * refls + k][c, p + j] = value


def add_kernel(a, b, out):
    out[...] = a[...] + b[...]


def final_kernel(refls, splits, place, params, *refs):
    amp, sup, lapped = refs[:3]
    own, mate = refs[3 : 3 + splits], refs[3 + splits : 3 + 2 * splits]
    others = refs[3 + 2 * splits : 3 + (1 + refls) * splits]
    phases = refs[3 + (1 + refls) * splits : -2]
    out_amp, out_disp = refs[-2:]
    planes, rows, depth = amp.shape
    first = pl.multiple_of(place[2] * rows, rows)
    portion = planes // splits

    for part in range(splits):

        def plane(i, carry, part=part):
            p = part * portion + i
            mask = sup[p, pl.ds(first, rows), :].astype(F32)
            weight = mask * amp[p]
            total = jnp.zeros((rows, depth), F32)
            moved = [jnp.zeros((rows, depth), F32) for _ in range(3)]
            for k in range(refls):
                if k == 0:
                    real, imag = [own[part][c, i] + mate[part][c, i] for c in range(2)]
                else:
                    real, imag = [others[(k - 1) * splits + part][c, i] for c in range(2)]
                cosine, sine = phases[k][0, p], phases[k][1, p]
                total = total + (real * cosine + imag * sine)
                across = weight * (imag * cosine - real * sine)
                moved = [m + params[4 * k + c] * across for c, m in enumerate(moved)]
            out_amp[p] = mask * total + (2.0 * EDGE_WEIGHT) * (mask * lapped[0, p])
            for c in range(3):
                out_disp[c, p] = moved[c] + (2.0 * STRAIN_WEIGHT) * lapped[c + 1, p]
            return carry

        lax.fori_loop(0, portion, plane, 0)


def swap(x, axis, bits):
    count = lax.axis_size(axis)
    return lax.ppermute(x, axis, [(i, i ^ bits) for i in range(count)])


def swap_outward(x, axis):
    count = lax.axis_size(axis)
    return lax.ppermute(x, axis, [pair for i in range(1, count - 1, 2) for pair in ((i, i + 1), (i + 1, i))])


def step_up(x, axis):
    return lax.ppermute(x, axis, [(i, i + 1) for i in range(lax.axis_size(axis) - 1)])


def step_down(x, axis):
    return lax.ppermute(x, axis, [(i + 1, i) for i in range(lax.axis_size(axis) - 1)])


def after(value, *first):
    return lax.optimization_barrier((value, first))[0]


def body(amplitude, displacement, support, miller, shift_kz, intensity):
    refls = lax.axis_size("refl")
    slabs = lax.axis_size("slab")
    chips = slabs // 2
    planes, rows, depth = amplitude.shape
    edge = planes * slabs
    grid = 2 * edge
    keys = grid // slabs
    pieces = PIECES if sum(PIECES) == keys else (keys,)
    splits = 2 if planes % 8 == 0 else 1
    portion = planes // splits
    group = 2 * planes
    refl = lax.axis_index("refl")
    slab = lax.axis_index("slab")
    place = jnp.stack([slab // 2, slab % 2, refl]).astype(jnp.int32)
    cells = planes * rows * depth
    part_shape = (2, portion, rows, depth)

    every, inner = np.arange(grid), np.arange(edge)
    table = forward_table(every, inner, grid)
    constants = [jnp.asarray(t) for one in (table, table.T) for t in split_table(one)]
    by_key = table.reshape(2, chips, 2, keys, 2 * edge).transpose(2, 1, 3, 0, 4)

    def y_tables(at):
        first, count = sum(pieces[:at]), pieces[at]
        some = by_key[:, :, first : first + count].reshape(2, chips * count * 2, 2 * edge)
        fwd = [jnp.asarray(t) for t in split_table(some)]
        some = some.reshape(2, chips * count * 2, 2, refls, rows)
        some = some.transpose(0, 3, 2, 4, 1).reshape(2, 2 * edge, chips * count * 2)
        return fwd, [jnp.asarray(t) for t in split_table(some)]

    own_params = jnp.concatenate([miller[0].astype(F32), shift_kz.astype(F32)])
    fields = (amplitude, displacement, support)
    edges = call(
        edges_kernel, [(4, rows, depth)] * 2 + [(4, planes, depth)] * 2, [place], fields, [], cells, "edges"
    )

    def make(params, which, parts):
        made = call(
            functools.partial(object_kernel, which, grid),
            ([(2, planes, rows, depth)] + [(2, planes // parts, rows, depth)] * parts) * len(which),
            [place, params],
            fields,
            [],
            50 * len(which) * cells,
            "object",
        )
        return [made[i * (parts + 1) : (i + 1) * (parts + 1)] for i in range(len(which))]

    ((own_phase, *own_parts),) = make(own_params, [0], splits)
    params = jnp.concatenate([own_params] + [swap(own_params, "refl", k) for k in range(1, refls)])
    params = after(params, own_parts, edges)
    made = make(params, list(range(1, refls)), splits)
    phases = [own_phase] + [one[0] for one in made]
    own_mates = [swap(x, "slab", 1) for x in own_parts]
    held = [[swap(one[1], "refl", k + 1) for k, one in enumerate(made)]]
    if refls == 2:
        facing = swap(jnp.where(refl == 0, edges[3], edges[2]), "refl", 1)
        nothing = jnp.zeros_like(facing)
        y_halos = (jnp.where(refl == 0, nothing, facing), jnp.where(refl == 0, facing, nothing))
    else:
        y_halos = (step_up(edges[3], "refl"), step_down(edges[2], "refl"))
    halos = (swap(edges[0], "slab", 1), swap_outward(edges[1], "slab"), *y_halos)
    for part in range(1, splits):
        held.append([swap(after(one[1 + part], halos), "refl", k + 1) for k, one in enumerate(made)])

    held = [x for part in zip(*held) for x in part]
    mates = [swap(x, "slab", 1) for x in held]

    def y_forward(at):
        return call(
            functools.partial(y_forward_kernel, refls, chips, splits),
            [(group, 2 * pieces[at], depth)] * chips,
            [place],
            (*own_parts, *held, *own_mates, *mates, *y_tables(at)[0]),
            [pltpu.VMEM((2 * edge, group * depth), BF16)] * 2,
            6 * group * depth * 2 * edge * chips * pieces[at] * 2,
            "y_forward",
        )

    def middle(at, got):
        first, count = sum(pieces[:at]), pieces[at]
        block = (group, 2 * count, depth)
        held = min(keys, max(8, count))
        return call(
            functools.partial(middle_kernel, chips, first % held),
            [block] * chips,
            [place],
            (*got, intensity, *constants),
            [pltpu.VMEM((2 * edge, min(count, 4) * depth), F32)] * 2,
            6 * count * (2 * edge * 2 * grid * depth * 2 + grid * 2 * depth * 2 * grid * 2),
            "middle",
            {chips: ((1, grid, held, grid), (0, 0, first // held, 0))},
        )

    def y_adjoint(at, got, jobs, adds):
        count = pieces[at]
        made = call(
            functools.partial(y_adjoint_kernel, refls, chips, jobs),
            [part_shape] * (refls * len(jobs)),
            [place],
            (*got, *y_tables(at)[1], *[x for job in adds for x in job]),
            [pltpu.VMEM((chips * 2 * count, len(jobs) * portion * depth), F32)],
            6 * len(jobs) * portion * depth * 2 * edge * chips * 2 * count,
            "y_adjoint",
        )
        return [made[i * refls : (i + 1) * refls] for i in range(len(jobs))]

    def cross(sends, late=(), first=()):
        got = [sends[0]] + [None] * (chips - 1)
        for k in ORDER if len(ORDER) == chips - 1 else range(1, chips):
            got[k] = swap(after(sends[k], first) if k in late else sends[k], "slab", 2 * k)
        return got

    forward = [y_forward(at) for at in range(len(pieces))]
    arrived = cross(forward[0])
    (lapped,) = call(laplace_kernel, [(4, planes, rows, depth)], [place], (*fields, *halos), [], 30 * cells, "laplace")
    jobs = [(mate, part * portion) for part in range(splits) for mate in (True, False)]
    adds = []
    for at in range(len(pieces)):
        backs = middle(at, arrived)
        if at + 1 < len(pieces):
            arrived = cross(forward[at + 1], LATE, backs)
        returned = cross(backs)
        if at + 1 < len(pieces):
            adds = y_adjoint(at, returned, jobs, adds)
    own, mates, others = [], [], [[] for _ in range(1, refls)]
    mate_jobs = [job for job in range(len(jobs)) if jobs[job][0]]
    mine_jobs = [job for job in range(len(jobs)) if not jobs[job][0]]
    for_mate = y_adjoint(at, returned, [jobs[i] for i in mate_jobs], [adds[i] for i in mate_jobs if adds])
    mine = y_adjoint(at, returned, [jobs[i] for i in mine_jobs], [adds[i] for i in mine_jobs if adds])
    for part in range(splits):
        from_mate = [swap(x, "slab", 1) for x in for_mate[part]]
        own.append(mine[part][0])
        mates.append(from_mate[0])
        for k in range(1, refls):
            (total,) = call(add_kernel, [part_shape], [], (mine[part][k], from_mate[k]), [], 2 * cells, "add")
            others[k - 1].append(swap(total, "refl", k))
    others = [x for one in others for x in one]

    return tuple(
        call(
            functools.partial(final_kernel, refls, splits),
            [(planes, rows, depth), (3, planes, rows, depth)],
            [place, params],
            (amplitude, support, lapped, *own, *mates, *others, *phases),
            [],
            20 * refls * cells,
            "final",
        )
    )


def solution(mesh):
    placed = (
        P("slab", "refl", None),
        P(None, "slab", "refl", None),
        P("slab", None, None),
        P("refl", None),
        P("refl"),
        P("refl", None, "slab", None),
    )
    return jax.shard_map(
        body,
        mesh=mesh,
        in_specs=placed,
        out_specs=(P("slab", "refl", None), P(None, "slab", "refl", None)),
        check_vma=False,
    )
```

```python
import functools

import jax
import jax.numpy as jnp
import ml_dtypes
import numpy as np
from jax import lax
from jax.experimental import pallas as pl
from jax.experimental.pallas import tpu as pltpu
from jax.sharding import PartitionSpec as P

STRAIN_WEIGHT = 0.05
EDGE_WEIGHT = 0.05
PIECES = (8, 8)
F32 = jnp.float32
BF16 = jnp.bfloat16


def split_table(table):
    high = table.astype(ml_dtypes.bfloat16)
    low = (table - high.astype(np.float64)).astype(ml_dtypes.bfloat16)
    return high, low


def forward_table(freqs, places, length):
    angle = 2.0 * np.pi / length * (freqs[:, None] * places[None, :] % length)
    cosine = np.cos(angle) * length ** (-0.5)
    sine = np.sin(angle) * length ** (-0.5)
    return np.block([[cosine, sine], [-sine, cosine]])


def turn_fits():
    nodes = np.cos(np.pi * (np.arange(400) + 0.5) / 400)
    t = (nodes + 1.0) / 8.0
    r = np.sqrt(t)
    fits = []
    for values, degree in ((np.cos(2 * np.pi * r), 8), (np.sin(2 * np.pi * r) / r, 8)):
        cheb = np.polynomial.chebyshev.Chebyshev.fit(t, values, degree, domain=[0.0, 0.25])
        fits.append([float(c) for c in cheb.convert(kind=np.polynomial.Polynomial).coef])
    return fits


COS_FIT, SIN_FIT = turn_fits()


def series(coefs, t):
    total = jnp.full_like(t, coefs[-1])
    for coef in coefs[-2::-1]:
        total = total * t + coef
    return total


def halves(x):
    high = x.astype(BF16)
    return high, (x - high.astype(F32)).astype(BF16)


def dot(a, b):
    return jnp.dot(a, b, preferred_element_type=F32)


def dot_pairs(a, b):
    return dot(a[0], b[0]) + (dot(a[0], b[1]) + dot(a[1], b[0]))


SMEM = pl.BlockSpec(memory_space=pltpu.SMEM)


def whole(shape):
    return pl.BlockSpec(tuple(shape), lambda step, rank=len(shape): (0,) * rank)


def call(kernel, outs, scalars, operands, scratch, flops, name, blocks=None, first=(), vmem=48):
    blocks = blocks or {}
    inputs = len(scalars) + len(operands)
    specs = [SMEM] * len(scalars)
    moved = 4 * sum(int(np.prod(shape)) for shape in outs)
    for at, operand in enumerate(operands):
        if at in blocks and blocks[at] is None:
            shape = (0,)
            specs.append(pl.BlockSpec(memory_space=pl.ANY))
        elif at in blocks:
            shape, index = blocks[at]
            specs.append(pl.BlockSpec(shape, lambda step, index=index: index))
        else:
            shape = operand.shape
            specs.append(whole(shape))
        moved += int(np.prod(shape)) * operand.dtype.itemsize
    specs += [pl.BlockSpec(memory_space=pl.ANY)] * len(first)

    def run(*refs):
        kernel(*refs[:inputs], *refs[inputs + len(first) :])

    return pl.pallas_call(
        run,
        grid=(1,),
        out_shape=[jax.ShapeDtypeStruct(shape, F32) for shape in outs],
        in_specs=specs,
        out_specs=[whole(shape) for shape in outs],
        scratch_shapes=scratch,
        compiler_params=pltpu.CompilerParams(vmem_limit_bytes=vmem * 1024 * 1024),
        cost_estimate=pl.CostEstimate(flops=int(flops), bytes_accessed=int(moved), transcendentals=0),
        name=name,
    )(*scalars, *operands, *first)


def field_of(place, amp, disp, sup, f, p):
    if f > 0:
        return disp[f - 1, p]
    rows = amp.shape[1]
    return sup[p, pl.ds(pl.multiple_of(place[2] * rows, rows), rows), :].astype(F32) * amp[p]


def edges_kernel(place, amp, disp, sup, x_mate, x_out):
    planes = amp.shape[0]
    core = place[1]
    for f in range(4):
        x_mate[f] = field_of(place, amp, disp, sup, f, (1 - core) * (planes - 1))
        x_out[f] = field_of(place, amp, disp, sup, f, core * (planes - 1))


def pack_kernel(edged, place, a, b, amp, disp, sup, out):
    portion, rows, depth = a.shape[1:]
    planes = amp.shape[0]
    for c in range(2):
        for p in range(portion):
            at = (c * portion + p) * rows
            out[at : at + rows, :] = a[c, p] + b[c, p]
    if edged:
        for f in range(4):
            for p in range(planes):
                value = field_of(place, amp, disp, sup, f, p)
                at = 2 * portion * rows + f * planes + p
                out[at : at + 1, :] = value[:1]
                at += 4 * planes
                out[at : at + 1, :] = value[rows - 1 :]


def laplace_kernel(refls, place, amp, disp, sup, x_mate, x_out, *refs):
    planes, rows, depth = amp.shape
    packs, out = refs[:-1], refs[-1]
    refl = place[2]
    low_core = place[1] == 0
    row = lax.broadcasted_iota(jnp.int32, (rows, depth), 0)
    lane = lax.broadcasted_iota(jnp.int32, (rows, depth), 1)
    for f in range(4):
        for p in range(planes):
            centre = field_of(place, amp, disp, sup, f, p)
            before, behind = jnp.zeros((1, depth), F32), jnp.zeros((1, depth), F32)
            for k in range(1, refls):
                at = packs[k - 1].shape[0] - 8 * planes + f * planes + p
                behind = jnp.where((refl ^ k) - refl == 1, packs[k - 1][at : at + 1, :], behind)
                at += 4 * planes
                before = jnp.where(refl - (refl ^ k) == 1, packs[k - 1][at : at + 1, :], before)
            if p == 0:
                beside = jnp.where(low_core, x_out[f], x_mate[f])
            else:
                beside = field_of(place, amp, disp, sup, f, p - 1)
            if p == planes - 1:
                beside = beside + jnp.where(low_core, x_mate[f], x_out[f])
            else:
                beside = beside + field_of(place, amp, disp, sup, f, p + 1)
            beside = beside + jnp.where(row == 0, before, pltpu.roll(centre, 1, 0))
            beside = beside + jnp.where(row == rows - 1, behind, pltpu.roll(centre, rows - 1, 0))
            beside = beside + jnp.where(lane == 0, 0.0, pltpu.roll(centre, 1, 1))
            beside = beside + jnp.where(lane == depth - 1, 0.0, pltpu.roll(centre, depth - 1, 1))
            out[f, p] = 6.0 * centre - beside


def object_kernel(which, grid, place, params, amp, disp, sup, *outs):
    planes, rows, depth = amp.shape
    first = pl.multiple_of(place[2] * rows, rows)
    zed = lax.broadcasted_iota(jnp.int32, (rows, depth), 1).astype(F32) * (1.0 / grid)
    each = len(outs) // len(which)
    portion = planes // (each - 1)

    for part in range(each - 1):

        def plane(i, carry, part=part):
            p = part * portion + i
            weight = sup[p, pl.ds(first, rows), :].astype(F32) * amp[p]
            parts = [disp[0, p], disp[1, p], disp[2, p]]
            for at, k in enumerate(which):
                phase = params[4 * k] * parts[0] + params[4 * k + 1] * parts[1] + params[4 * k + 2] * parts[2]
                shifted = params[4 * k + 3] * zed
                turns = phase * (0.5 / np.pi) + (shifted - jnp.floor(shifted))
                turns = turns - jnp.floor(turns + 0.5)
                square = turns * turns
                cosine = series(COS_FIT, square)
                sine = series(SIN_FIT, square) * turns
                outs[each * at][0, p] = cosine
                outs[each * at][1, p] = sine
                outs[each * at + 1 + part][0, i] = weight * cosine
                outs[each * at + 1 + part][1, i] = weight * sine
            return carry

        lax.fori_loop(0, portion, plane, 0)


def y_forward_kernel(refls, chips, splits, targets, place, *refs):
    count = 2 * refls * splits
    parts, tables, outs = refs[:count], refs[count], refs[count + 1 : -2]
    hold_high, hold_low = refs[-2:]
    chip, core, refl = place[0], place[1], place[2]
    portion, rows, depth = parts[0].shape[1:]
    planes = portion * splits
    length = rows * refls
    share = tables.shape[2] // chips

    def order(which):
        return jnp.concatenate(
            [tables[core, which, pl.ds(pl.multiple_of((chip ^ k) * share, share), share), :] for k in targets],
            axis=0,
        )

    table = (order(0), order(1))
    for src in range(2):
        for p in range(planes):
            lane = (src * planes + p) * depth
            for c in range(2):
                for k in range(refls):
                    part = parts[(src * refls + k) * splits + p // portion]
                    one, two = halves(part[c, p % portion])
                    at = pl.ds(pl.multiple_of(c * length + (refl ^ k) * rows, rows), rows)
                    hold_high[at, lane : lane + depth] = one
                    hold_low[at, lane : lane + depth] = two
    for src in range(2):
        for p in range(0, planes, 2):
            lane = (src * planes + p) * depth
            operand = (hold_high[:, lane : lane + 2 * depth], hold_low[:, lane : lane + 2 * depth])
            result = dot_pairs(table, operand)
            base = (core if src == 0 else 1 - core) * planes + p
            for i in range(len(targets)):
                for j in range(2):
                    outs[i][base + j] = result[i * share : (i + 1) * share, j * depth : (j + 1) * depth]


def middle_kernel(chips, first, place, *refs):
    got, intensity = refs[:chips], refs[chips]
    fwd = (refs[chips + 1][...], refs[chips + 2][...])
    bwd = (refs[chips + 3][...], refs[chips + 4][...])
    outs = refs[chips + 5 : -4]
    gather, scatter, measured, arrived = refs[-4:]
    chip = place[0]
    group, width, depth = got[0].shape
    rows = width // 2
    edge = group * chips
    grid = 2 * edge
    batch = gather.shape[1] // depth
    load = pltpu.make_async_copy(intensity.at[0, :, first : first + rows, :], measured, arrived)
    load.start()

    def place_of(c, k):
        return pl.ds(pl.multiple_of(c * edge + (chip ^ k) * group, group), group)

    for key in range(0, rows, batch):
        for k in range(chips):
            for c in range(2):
                for j in range(batch):
                    gather[place_of(c, k), j * depth : (j + 1) * depth] = got[k][:, (key + j) * 2 + c, :]
        one = dot_pairs(fwd, halves(gather[...]))
        if key == 0:
            load.wait()
        back = []
        for j in range(batch):
            lines = [one[c * grid : (c + 1) * grid, j * depth : (j + 1) * depth] for c in range(2)]
            spectrum = dot_pairs(halves(jnp.concatenate(lines, axis=1)), bwd)
            real, imag = spectrum[:, :grid], spectrum[:, grid:]
            excess = 4.0 * (real * real + imag * imag - measured[:, key + j, :])
            back.append(dot_pairs(halves(jnp.concatenate([excess * real, excess * imag], axis=1)), fwd))
        lines = [jnp.concatenate([b[:, c * depth : (c + 1) * depth] for b in back], axis=1) for c in range(2)]
        scatter[...] = dot_pairs(bwd, halves(jnp.concatenate(lines, axis=0)))
        for k in range(chips):
            for c in range(2):
                for j in range(batch):
                    outs[k][:, (key + j) * 2 + c, :] = scatter[place_of(c, k), j * depth : (j + 1) * depth]


def y_adjoint_kernel(refls, chips, jobs, place, *refs):
    got, tables = refs[:chips], refs[chips]
    total = refls * len(jobs)
    adds, outs = refs[chips + 1 : -2 - total], refs[-2 - total : -2]
    done, hold = refs[-2:]
    done[...] = jnp.zeros_like(done)
    chip, core, refl = place[0], place[1], place[2]
    planes, rows, depth = outs[0].shape[1:]
    width = got[0].shape[1]

    def order(which):
        pieces = []
        for q in range(refls):
            for c in range(2):
                at = pl.multiple_of(((refl ^ q) * 2 + c) * rows, rows)
                pieces.append(tables[core, which, pl.ds(at, rows), :])
        return jnp.concatenate(pieces, axis=0)

    table = (order(0), order(1))
    for job, (mate, first) in enumerate(jobs):
        base = (1 - core if mate else core) * (got[0].shape[0] // 2) + first
        for p in range(planes):
            lane = (job * planes + p) * depth
            for k in range(chips):
                at = pl.ds(pl.multiple_of((chip ^ k) * width, width), width)
                hold[at, lane : lane + depth] = got[k][base + p]
    for job in range(len(jobs)):
        for p in range(0, planes, 2):
            lane = (job * planes + p) * depth
            result = dot_pairs(table, halves(hold[:, lane : lane + 2 * depth]))
            for k in range(refls):
                for c in range(2):
                    at = (k * 2 + c) * rows
                    for j in range(2):
                        value = result[at : at + rows, j * depth : (j + 1) * depth]
                        if adds:
                            value = value + adds[job * refls + k][c, p + j]
                        outs[job * refls + k][c, p + j] = value


def final_kernel(refls, splits, place, params, *refs):
    amp, sup, lapped = refs[:3]
    own, mate = refs[3 : 3 + splits], refs[3 + splits : 3 + 2 * splits]
    others = refs[3 + 2 * splits : 3 + (1 + refls) * splits]
    phases = refs[3 + (1 + refls) * splits : -2]
    out_amp, out_disp = refs[-2:]
    planes, rows, depth = amp.shape
    first = pl.multiple_of(place[2] * rows, rows)
    portion = planes // splits

    for part in range(splits):

        def plane(i, carry, part=part):
            p = part * portion + i
            mask = sup[p, pl.ds(first, rows), :].astype(F32)
            weight = mask * amp[p]
            total = jnp.zeros((rows, depth), F32)
            moved = [jnp.zeros((rows, depth), F32) for _ in range(3)]
            for k in range(refls):
                if k == 0:
                    real, imag = [own[part][c, i] + mate[part][c, i] for c in range(2)]
                else:
                    at = [pl.ds(pl.multiple_of((c * portion + i) * rows, rows), rows) for c in range(2)]
                    real, imag = [others[(k - 1) * splits + part][at[c], :] for c in range(2)]
                cosine, sine = phases[k][0, p], phases[k][1, p]
                total = total + (real * cosine + imag * sine)
                across = weight * (imag * cosine - real * sine)
                moved = [m + params[4 * k + c] * across for c, m in enumerate(moved)]
            out_amp[p] = mask * total + (2.0 * EDGE_WEIGHT) * (mask * lapped[0, p])
            for c in range(3):
                out_disp[c, p] = moved[c] + (2.0 * STRAIN_WEIGHT) * lapped[c + 1, p]
            return carry

        lax.fori_loop(0, portion, plane, 0)


def swap(x, axis, bits):
    count = lax.axis_size(axis)
    return lax.ppermute(x, axis, [(i, i ^ bits) for i in range(count)])


def swap_outward(x, axis):
    count = lax.axis_size(axis)
    return lax.ppermute(x, axis, [pair for i in range(1, count - 1, 2) for pair in ((i, i + 1), (i + 1, i))])


def body(amplitude, displacement, support, miller, shift_kz, intensity):
    refls = lax.axis_size("refl")
    slabs = lax.axis_size("slab")
    chips = slabs // 2
    planes, rows, depth = amplitude.shape
    edge = planes * slabs
    grid = 2 * edge
    keys = grid // slabs
    pieces = PIECES if sum(PIECES) == keys else (keys,)
    splits = 2 if planes % 8 == 0 else 1
    portion = planes // splits
    group = 2 * planes
    refl = lax.axis_index("refl")
    slab = lax.axis_index("slab")
    place = jnp.stack([slab // 2, slab % 2, refl]).astype(jnp.int32)
    cells = planes * rows * depth
    part_shape = (2, portion, rows, depth)

    every, inner = np.arange(grid), np.arange(edge)
    table = forward_table(every, inner, grid)
    constants = [jnp.asarray(t) for one in (table, table.T) for t in split_table(one)]
    by_key = table.reshape(2, chips, 2, keys, 2 * edge).transpose(2, 1, 3, 0, 4)

    def y_tables(at):
        first, count = sum(pieces[:at]), pieces[at]
        some = by_key[:, :, first : first + count].reshape(2, chips * count * 2, 2 * edge)
        fwd = jnp.asarray(np.stack(split_table(some), axis=1))
        some = some.reshape(2, chips * count * 2, 2, refls, rows)
        some = some.transpose(0, 3, 2, 4, 1).reshape(2, 2 * edge, chips * count * 2)
        return fwd, jnp.asarray(np.stack(split_table(some), axis=1))

    own_params = jnp.concatenate([miller[0].astype(F32), shift_kz.astype(F32)])
    fields = (amplitude, displacement, support)
    def make(params, which, parts, vmem=48):
        made = call(
            functools.partial(object_kernel, which, grid),
            ([(2, planes, rows, depth)] + [(2, planes // parts, rows, depth)] * parts) * len(which),
            [place, params],
            fields,
            [],
            50 * len(which) * cells,
            "object",
            vmem=vmem,
        )
        return [made[i * (parts + 1) : (i + 1) * (parts + 1)] for i in range(len(which))]

    ((own_phase, *own_parts),) = make(own_params, [0], splits)
    params = jnp.concatenate([own_params] + [swap(own_params, "refl", k) for k in range(1, refls)])
    made = make(params, list(range(1, refls)), splits, vmem=60)
    phases = [own_phase] + [one[0] for one in made]
    own_mates = [swap(x, "slab", 1) for x in own_parts]
    held = [[swap(one[1], "refl", k + 1) for k, one in enumerate(made)]]
    for part in range(1, splits):
        held.append([swap(one[1 + part], "refl", k + 1) for k, one in enumerate(made)])

    held = [x for part in zip(*held) for x in part]
    mates = [swap(x, "slab", 1) for x in held]

    def y_forward(at, targets, first=()):
        made = call(
            functools.partial(y_forward_kernel, refls, chips, splits, targets),
            [(group, 2 * pieces[at], depth)] * len(targets),
            [place],
            (*own_parts, *held, *own_mates, *mates, y_tables(at)[0]),
            [pltpu.VMEM((2 * edge, group * depth), BF16)] * 2,
            6 * group * depth * 2 * edge * len(targets) * pieces[at] * 2,
            "y_forward",
            first=first,
        )
        return dict(zip(targets, made))

    def middle(at, got, first=()):
        count = pieces[at]
        return call(
            functools.partial(middle_kernel, chips, sum(pieces[:at])),
            [(group, 2 * count, depth)] * chips,
            [place],
            (*got, intensity, *constants),
            [pltpu.VMEM((2 * edge, min(count, 8) * depth), F32)] * 2
            + [pltpu.VMEM((grid, count, grid), F32), pltpu.SemaphoreType.DMA],
            6 * count * (2 * edge * 2 * grid * depth * 2 + grid * 2 * depth * 2 * grid * 2),
            "middle",
            {chips: None},
            first,
        )

    def y_adjoint(at, got, jobs, adds, first=()):
        count = pieces[at]
        made = call(
            functools.partial(y_adjoint_kernel, refls, chips, jobs),
            [part_shape] * (refls * len(jobs)) + [(8, 128)],
            [place],
            (*got, y_tables(at)[1], *[x for job in adds for x in job]),
            [pltpu.VMEM((chips * 2 * count, len(jobs) * portion * depth), F32)],
            6 * len(jobs) * portion * depth * 2 * edge * chips * 2 * count,
            "y_adjoint",
            first=first,
        )
        return [made[i * refls : (i + 1) * refls] for i in range(len(jobs))], made[-1]

    def cross(sends):
        return [sends[0]] + [swap(sends[k], "slab", 2 * k) for k in range(1, chips)]

    sends = [y_forward(at, list(range(chips))) for at in range(len(pieces))]
    jobs = [(mate, part * portion) for part in range(splits) for mate in (True, False)]
    adds = []
    for at in range(len(pieces)):
        backs = middle(at, cross(sends[at]))
        returned = cross(backs)
        if at + 1 < len(pieces):
            adds, unused = y_adjoint(at, returned, jobs, adds)
    sums = []
    own, mates, others = [], [], [[] for _ in range(1, refls)]
    mate_jobs = [job for job in range(len(jobs)) if jobs[job][0]]
    mine_jobs = [job for job in range(len(jobs)) if not jobs[job][0]]
    for_mate, first_done = y_adjoint(at, returned, [jobs[i] for i in mate_jobs], [adds[i] for i in mate_jobs if adds])
    mine, unused = y_adjoint(at, returned, [jobs[i] for i in mine_jobs], [adds[i] for i in mine_jobs if adds], (first_done,))
    for part in range(splits):
        from_mate = [swap(x, "slab", 1) for x in for_mate[part]]
        own.append(mine[part][0])
        mates.append(from_mate[0])
        for k in range(1, refls):
            shape = (2 * portion * rows + (8 * planes if part == 0 else 0), depth)
            (total,) = call(
                functools.partial(pack_kernel, part == 0),
                [shape],
                [place],
                (mine[part][k], from_mate[k], *fields),
                [],
                4 * cells,
                "pack",
            )
            sums.append(total)
            others[k - 1].append(swap(total, "refl", k))
    edges = call(edges_kernel, [(4, rows, depth)] * 2, [place], fields, [], cells, "edges", first=sums)
    halos = (swap(edges[0], "slab", 1), swap_outward(edges[1], "slab"), *[one[0] for one in others])
    (lapped,) = call(
        functools.partial(laplace_kernel, refls),
        [(4, planes, rows, depth)],
        [place],
        (*fields, *halos),
        [],
        30 * cells,
        "laplace",
    )
    others = [x for one in others for x in one]

    return tuple(
        call(
            functools.partial(final_kernel, refls, splits),
            [(planes, rows, depth), (3, planes, rows, depth)],
            [place, params],
            (amplitude, support, lapped, *own, *mates, *others, *phases),
            [],
            20 * refls * cells,
            "final",
        )
    )


def solution(mesh):
    placed = (
        P("slab", "refl", None),
        P(None, "slab", "refl", None),
        P("slab", None, None),
        P("refl", None),
        P("refl"),
        P("refl", None, "slab", None),
    )
    return jax.shard_map(
        body,
        mesh=mesh,
        in_specs=placed,
        out_specs=(P("slab", "refl", None), P(None, "slab", "refl", None)),
        check_vma=False,
    )
```

```python
import functools

import jax
import jax.numpy as jnp
import ml_dtypes
import numpy as np
from jax import lax
from jax.experimental import pallas as pl
from jax.experimental.pallas import tpu as pltpu
from jax.sharding import PartitionSpec as P

STRAIN_WEIGHT = 0.05
EDGE_WEIGHT = 0.05
PIECES = (8, 8)
F32 = jnp.float32
BF16 = jnp.bfloat16


def split_table(table):
    high = table.astype(ml_dtypes.bfloat16)
    low = (table - high.astype(np.float64)).astype(ml_dtypes.bfloat16)
    return high, low


def forward_table(freqs, places, length):
    angle = 2.0 * np.pi / length * (freqs[:, None] * places[None, :] % length)
    cosine = np.cos(angle) * length ** (-0.5)
    sine = np.sin(angle) * length ** (-0.5)
    return np.block([[cosine, sine], [-sine, cosine]])


def turn_fits():
    nodes = np.cos(np.pi * (np.arange(400) + 0.5) / 400)
    t = (nodes + 1.0) / 8.0
    r = np.sqrt(t)
    fits = []
    for values, degree in ((np.cos(2 * np.pi * r), 8), (np.sin(2 * np.pi * r) / r, 8)):
        cheb = np.polynomial.chebyshev.Chebyshev.fit(t, values, degree, domain=[0.0, 0.25])
        fits.append([float(c) for c in cheb.convert(kind=np.polynomial.Polynomial).coef])
    return fits


COS_FIT, SIN_FIT = turn_fits()


def series(coefs, t):
    total = jnp.full_like(t, coefs[-1])
    for coef in coefs[-2::-1]:
        total = total * t + coef
    return total


def halves(x):
    high = x.astype(BF16)
    return high, (x - high.astype(F32)).astype(BF16)


def dot(a, b):
    return jnp.dot(a, b, preferred_element_type=F32)


def dot_pairs(a, b):
    return dot(a[0], b[0]) + (dot(a[0], b[1]) + dot(a[1], b[0]))


SMEM = pl.BlockSpec(memory_space=pltpu.SMEM)


def whole(shape):
    return pl.BlockSpec(tuple(shape), lambda step, rank=len(shape): (0,) * rank)


def call(kernel, outs, scalars, operands, scratch, flops, name, blocks=None, first=(), vmem=48, out_blocks=None, carried=()):
    blocks = blocks or {}
    inputs = len(scalars) + len(operands)
    specs = [SMEM] * len(scalars)
    moved = 4 * sum(int(np.prod(shape)) for shape in outs)
    for at, operand in enumerate(operands):
        if at in blocks and blocks[at] is None:
            shape = (0,)
            specs.append(pl.BlockSpec(memory_space=pl.ANY))
        elif at in blocks:
            shape, index = blocks[at]
            specs.append(pl.BlockSpec(shape, lambda step, index=index: index))
        else:
            shape = operand.shape
            specs.append(whole(shape))
        moved += int(np.prod(shape)) * operand.dtype.itemsize
    first = (*first, *carried)
    specs += [pl.BlockSpec(memory_space=pl.ANY)] * len(first)
    aliases = {len(specs) - len(carried) + i: i for i in range(len(carried))}

    def run(*refs):
        kernel(*refs[:inputs], *refs[inputs + len(first) :])

    return pl.pallas_call(
        run,
        grid=(1,),
        out_shape=[jax.ShapeDtypeStruct(shape, F32) for shape in outs],
        in_specs=specs,
        out_specs=[
            pl.BlockSpec(shape, lambda step, index=index: index)
            for shape, index in out_blocks or [(shape, (0,) * len(shape)) for shape in outs]
        ],
        input_output_aliases=aliases,
        scratch_shapes=scratch,
        compiler_params=pltpu.CompilerParams(vmem_limit_bytes=vmem * 1024 * 1024),
        cost_estimate=pl.CostEstimate(flops=int(flops), bytes_accessed=int(moved), transcendentals=0),
        name=name,
    )(*scalars, *operands, *first)


def field_of(place, amp, disp, sup, f, p):
    if f > 0:
        return disp[f - 1, p]
    rows = amp.shape[1]
    return sup[p, pl.ds(pl.multiple_of(place[2] * rows, rows), rows), :].astype(F32) * amp[p]


def edges_kernel(place, amp, disp, sup, x_mate, x_out):
    planes = amp.shape[0]
    core = place[1]
    for f in range(4):
        x_mate[f] = field_of(place, amp, disp, sup, f, (1 - core) * (planes - 1))
        x_out[f] = field_of(place, amp, disp, sup, f, core * (planes - 1))


def pack_kernel(edged, place, a, b, amp, disp, sup, out):
    portion, rows, depth = a.shape[1:]
    planes = amp.shape[0]
    for c in range(2):
        for p in range(portion):
            at = (c * portion + p) * rows
            out[at : at + rows, :] = a[c, p] + b[c, p]
    if edged:
        for f in range(4):
            for p in range(planes):
                value = field_of(place, amp, disp, sup, f, p)
                at = 2 * portion * rows + f * planes + p
                out[at : at + 1, :] = value[:1]
                at += 4 * planes
                out[at : at + 1, :] = value[rows - 1 :]


def laplace_kernel(refls, place, amp, disp, sup, x_mate, x_out, *refs):
    planes, rows, depth = amp.shape
    packs, out = refs[:-1], refs[-1]
    refl = place[2]
    low_core = place[1] == 0
    row = lax.broadcasted_iota(jnp.int32, (rows, depth), 0)
    lane = lax.broadcasted_iota(jnp.int32, (rows, depth), 1)
    for f in range(4):
        for p in range(planes):
            centre = field_of(place, amp, disp, sup, f, p)
            before, behind = jnp.zeros((1, depth), F32), jnp.zeros((1, depth), F32)
            for k in range(1, refls):
                at = packs[k - 1].shape[0] - 8 * planes + f * planes + p
                behind = jnp.where((refl ^ k) - refl == 1, packs[k - 1][at : at + 1, :], behind)
                at += 4 * planes
                before = jnp.where(refl - (refl ^ k) == 1, packs[k - 1][at : at + 1, :], before)
            if p == 0:
                beside = jnp.where(low_core, x_out[f], x_mate[f])
            else:
                beside = field_of(place, amp, disp, sup, f, p - 1)
            if p == planes - 1:
                beside = beside + jnp.where(low_core, x_mate[f], x_out[f])
            else:
                beside = beside + field_of(place, amp, disp, sup, f, p + 1)
            beside = beside + jnp.where(row == 0, before, pltpu.roll(centre, 1, 0))
            beside = beside + jnp.where(row == rows - 1, behind, pltpu.roll(centre, rows - 1, 0))
            beside = beside + jnp.where(lane == 0, 0.0, pltpu.roll(centre, 1, 1))
            beside = beside + jnp.where(lane == depth - 1, 0.0, pltpu.roll(centre, depth - 1, 1))
            out[f, p] = 6.0 * centre - beside


def object_kernel(which, grid, place, *refs):
    params, (amp, disp, sup), outs = refs[: len(which)], refs[len(which) : len(which) + 3], refs[len(which) + 3 :]
    planes, rows, depth = amp.shape
    first = pl.multiple_of(place[2] * rows, rows)
    zed = lax.broadcasted_iota(jnp.int32, (rows, depth), 1).astype(F32) * (1.0 / grid)

    def plane(p, carry):
        weight = sup[p, pl.ds(first, rows), :].astype(F32) * amp[p]
        parts = [disp[0, p], disp[1, p], disp[2, p]]
        for at, param in enumerate(params):
            phase = param[0] * parts[0] + param[1] * parts[1] + param[2] * parts[2]
            shifted = param[3] * zed
            turns = phase * (0.5 / np.pi) + (shifted - jnp.floor(shifted))
            turns = turns - jnp.floor(turns + 0.5)
            square = turns * turns
            cosine = series(COS_FIT, square)
            sine = series(SIN_FIT, square) * turns
            outs[2 * at][0, p] = cosine
            outs[2 * at][1, p] = sine
            outs[2 * at + 1][0, p] = weight * cosine
            outs[2 * at + 1][1, p] = weight * sine
        return carry

    lax.fori_loop(0, planes, plane, 0)


def y_forward_kernel(refls, chips, splits, targets, place, *refs):
    count = 2 * refls * splits
    parts, tables, outs = refs[:count], refs[count], refs[count + 1 : -2]
    hold_high, hold_low = refs[-2:]
    chip, core, refl = place[0], place[1], place[2]
    portion, rows, depth = parts[0].shape[1:]
    planes = portion * splits
    length = rows * refls
    share = tables.shape[2] // chips

    def order(which):
        return jnp.concatenate(
            [tables[core, which, pl.ds(pl.multiple_of((chip ^ k) * share, share), share), :] for k in targets],
            axis=0,
        )

    table = (order(0), order(1))
    for src in range(2):
        for p in range(planes):
            lane = (src * planes + p) * depth
            for c in range(2):
                for k in range(refls):
                    part = parts[(src * refls + k) * splits + p // portion]
                    one, two = halves(part[c, p % portion])
                    at = pl.ds(pl.multiple_of(c * length + (refl ^ k) * rows, rows), rows)
                    hold_high[at, lane : lane + depth] = one
                    hold_low[at, lane : lane + depth] = two
    for src in range(2):
        for p in range(0, planes, 2):
            lane = (src * planes + p) * depth
            operand = (hold_high[:, lane : lane + 2 * depth], hold_low[:, lane : lane + 2 * depth])
            result = dot_pairs(table, operand)
            base = (core if src == 0 else 1 - core) * planes + p
            for i in range(len(targets)):
                for j in range(2):
                    outs[i][base + j] = result[i * share : (i + 1) * share, j * depth : (j + 1) * depth]


def middle_kernel(chips, first, place, *refs):
    got, intensity = refs[:chips], refs[chips]
    fwd = (refs[chips + 1][...], refs[chips + 2][...])
    bwd = (refs[chips + 3][...], refs[chips + 4][...])
    outs = refs[chips + 5 : -4]
    gather, scatter, measured, arrived = refs[-4:]
    chip = place[0]
    group, width, depth = got[0].shape
    rows = width // 2
    edge = group * chips
    grid = 2 * edge
    batch = gather.shape[1] // depth
    held = first // 8 * 8
    load = pltpu.make_async_copy(intensity.at[0, :, held : held + measured.shape[1], :], measured, arrived)
    load.start()

    def place_of(c, k):
        return pl.ds(pl.multiple_of(c * edge + (chip ^ k) * group, group), group)

    for key in range(0, rows, batch):
        for k in range(chips):
            for c in range(2):
                for j in range(batch):
                    gather[place_of(c, k), j * depth : (j + 1) * depth] = got[k][:, (key + j) * 2 + c, :]
        one = dot_pairs(fwd, halves(gather[...]))
        if key == 0:
            load.wait()
        back = []
        for j in range(batch):
            lines = [one[c * grid : (c + 1) * grid, j * depth : (j + 1) * depth] for c in range(2)]
            spectrum = dot_pairs(halves(jnp.concatenate(lines, axis=1)), bwd)
            real, imag = spectrum[:, :grid], spectrum[:, grid:]
            excess = 4.0 * (real * real + imag * imag - measured[:, first - held + key + j, :])
            back.append(dot_pairs(halves(jnp.concatenate([excess * real, excess * imag], axis=1)), fwd))
        lines = [jnp.concatenate([b[:, c * depth : (c + 1) * depth] for b in back], axis=1) for c in range(2)]
        scatter[...] = dot_pairs(bwd, halves(jnp.concatenate(lines, axis=0)))
        for k in range(chips):
            for c in range(2):
                for j in range(batch):
                    outs[k][:, (key + j) * 2 + c, :] = scatter[place_of(c, k), j * depth : (j + 1) * depth]


def y_adjoint_kernel(chips, jobs, parts, place, *refs):
    got, tables = refs[:chips], refs[chips]
    total = len(parts) * len(jobs)
    adds, outs = refs[chips + 1 : -2 - total], refs[-2 - total : -2]
    done, hold = refs[-2:]
    done[...] = jnp.zeros_like(done)
    chip, core, refl = place[0], place[1], place[2]
    planes, rows, depth = outs[0].shape[1:]
    width = got[0].shape[1]

    def order(which):
        pieces = []
        for q in parts:
            for c in range(2):
                at = pl.multiple_of(((refl ^ q) * 2 + c) * rows, rows)
                pieces.append(tables[core, which, pl.ds(at, rows), :])
        return jnp.concatenate(pieces, axis=0)

    table = (order(0), order(1))
    for job, (mate, first) in enumerate(jobs):
        base = (1 - core if mate else core) * (got[0].shape[0] // 2) + first
        for p in range(planes):
            lane = (job * planes + p) * depth
            for k in range(chips):
                at = pl.ds(pl.multiple_of((chip ^ k) * width, width), width)
                hold[at, lane : lane + depth] = got[k][base + p]
    for job in range(len(jobs)):
        for p in range(0, planes, 2):
            lane = (job * planes + p) * depth
            result = dot_pairs(table, halves(hold[:, lane : lane + 2 * depth]))
            for i in range(len(parts)):
                for c in range(2):
                    at = (i * 2 + c) * rows
                    for j in range(2):
                        value = result[at : at + rows, j * depth : (j + 1) * depth]
                        if adds:
                            value = value + adds[job * len(parts) + i][c, p + j]
                        outs[job * len(parts) + i][c, p + j] = value


def final_kernel(refls, place, *refs):
    params = refs[:refls]
    amp, sup, lapped, own, mate = refs[refls : refls + 5]
    others, phases = refs[refls + 5 : 2 * refls + 4], refs[2 * refls + 4 : -2]
    out_amp, out_disp = refs[-2:]
    planes, rows, depth = amp.shape
    first = pl.multiple_of(place[2] * rows, rows)

    def plane(p, carry):
        mask = sup[p, pl.ds(first, rows), :].astype(F32)
        weight = mask * amp[p]
        total = jnp.zeros((rows, depth), F32)
        moved = [jnp.zeros((rows, depth), F32) for _ in range(3)]
        for k in range(refls):
            if k == 0:
                real, imag = [own[c, p] + mate[c, p] for c in range(2)]
            else:
                at = [pl.ds(pl.multiple_of((c * planes + p) * rows, rows), rows) for c in range(2)]
                real, imag = [others[k - 1][at[c], :] for c in range(2)]
            cosine, sine = phases[k][0, p], phases[k][1, p]
            total = total + (real * cosine + imag * sine)
            across = weight * (imag * cosine - real * sine)
            moved = [m + params[k][c] * across for c, m in enumerate(moved)]
        out_amp[p] = mask * total + (2.0 * EDGE_WEIGHT) * (mask * lapped[0, p])
        for c in range(3):
            out_disp[c, p] = moved[c] + (2.0 * STRAIN_WEIGHT) * lapped[c + 1, p]
        return carry

    lax.fori_loop(0, planes, plane, 0)


def swap(x, axis, bits):
    count = lax.axis_size(axis)
    return lax.ppermute(x, axis, [(i, i ^ bits) for i in range(count)])


def swap_outward(x, axis):
    count = lax.axis_size(axis)
    return lax.ppermute(x, axis, [pair for i in range(1, count - 1, 2) for pair in ((i, i + 1), (i + 1, i))])


def body(amplitude, displacement, support, miller, shift_kz, intensity):
    refls = lax.axis_size("refl")
    slabs = lax.axis_size("slab")
    chips = slabs // 2
    planes, rows, depth = amplitude.shape
    edge = planes * slabs
    grid = 2 * edge
    keys = grid // slabs
    pieces = PIECES if sum(PIECES) == keys else (keys,)
    splits = 2 if planes % 8 == 0 else 1
    portion = planes // splits
    group = 2 * planes
    refl = lax.axis_index("refl")
    slab = lax.axis_index("slab")
    place = jnp.stack([slab // 2, slab % 2, refl]).astype(jnp.int32)
    cells = planes * rows * depth
    part_shape = (2, portion, rows, depth)

    every, inner = np.arange(grid), np.arange(edge)
    table = forward_table(every, inner, grid)
    constants = [jnp.asarray(t) for one in (table, table.T) for t in split_table(one)]
    by_key = table.reshape(2, chips, 2, keys, 2 * edge).transpose(2, 1, 3, 0, 4)

    def y_tables(at):
        first, count = sum(pieces[:at]), pieces[at]
        some = by_key[:, :, first : first + count].reshape(2, chips * count * 2, 2 * edge)
        fwd = jnp.asarray(np.stack(split_table(some), axis=1))
        some = some.reshape(2, chips * count * 2, 2, refls, rows)
        some = some.transpose(0, 3, 2, 4, 1).reshape(2, 2 * edge, chips * count * 2)
        return fwd, jnp.asarray(np.stack(split_table(some), axis=1))

    own_params = jnp.concatenate([miller[0].astype(F32), shift_kz.astype(F32)])
    fields = (amplitude, displacement, support)
    def part_blocks(part, start=0):
        return {
            start: ((portion, rows, depth), (part, 0, 0)),
            start + 1: ((3, portion, rows, depth), (0, part, 0, 0)),
            start + 2: ((portion, rows * refls, depth), (part, 0, 0)),
        }

    def make(part, which, vmem=48, first=()):
        made = call(
            functools.partial(object_kernel, which, grid),
            [part_shape] * (2 * len(which)),
            [place, *[params[k] for k in which]],
            fields,
            [],
            50 * len(which) * cells // splits,
            "object",
            part_blocks(part),
            first,
            vmem,
        )
        return {k: made[2 * i : 2 * i + 2] for i, k in enumerate(which)}

    params = [own_params] + [swap(own_params, "refl", k) for k in range(1, refls)]
    made = [make(0, list(range(1, refls)), 60)]
    made += [make(part, list(range(1, refls)), 60, [made[0][1][1]]) for part in range(1, splits)]
    held = [swap(made[part][k][1], "refl", k) for k in range(1, refls) for part in range(splits)]
    for part in range(splits):
        made[part].update(make(part, [0]))
    own_parts = [made[part][0][1] for part in range(splits)]
    own_mates = [swap(x, "slab", 1) for x in own_parts]
    mates = [swap(x, "slab", 1) for x in held]

    def y_forward(at, targets, first=()):
        made = call(
            functools.partial(y_forward_kernel, refls, chips, splits, targets),
            [(group, 2 * pieces[at], depth)] * len(targets),
            [place],
            (*own_parts, *held, *own_mates, *mates, y_tables(at)[0]),
            [pltpu.VMEM((2 * edge, group * depth), BF16)] * 2,
            6 * group * depth * 2 * edge * len(targets) * pieces[at] * 2,
            "y_forward",
            first=first,
        )
        return dict(zip(targets, made))

    def middle(at, got):
        first, count = sum(pieces[:at]), pieces[at]
        held = -(-(first + count) // 8) * 8 - first // 8 * 8
        return call(
            functools.partial(middle_kernel, chips, first),
            [(group, 2 * count, depth)] * chips,
            [place],
            (*got, intensity, *constants),
            [pltpu.VMEM((2 * edge, (count if count < 8 else count // 2 if count > 8 else 8) * depth), F32)] * 2
            + [pltpu.VMEM((grid, held, grid), F32), pltpu.SemaphoreType.DMA],
            6 * count * (2 * edge * 2 * grid * depth * 2 + grid * 2 * depth * 2 * grid * 2),
            "middle",
            {chips: None},
        )

    def y_adjoint(at, got, jobs, parts, adds=None, first=()):
        count = pieces[at]
        made = call(
            functools.partial(y_adjoint_kernel, chips, jobs, parts),
            [part_shape] * (len(parts) * len(jobs)) + [(8, 128)],
            [place],
            (*got, y_tables(at)[1], *([adds[job][k] for job in jobs for k in parts] if adds else [])),
            [pltpu.VMEM((chips * 2 * count, len(jobs) * portion * depth), F32)],
            6 * len(jobs) * portion * depth * len(parts) * 2 * rows * chips * 2 * count,
            "y_adjoint",
            first=first,
        )
        each = len(parts)
        return {job: dict(zip(parts, made[i * each : (i + 1) * each])) for i, job in enumerate(jobs)}, made[-1]

    def cross(sends):
        return [sends[0]] + [swap(sends[k], "slab", 2 * k) for k in range(1, chips)]

    sends = [y_forward(at, list(range(chips))) for at in range(len(pieces))]
    jobs = {mate: [(mate, part * portion) for part in range(splits)] for mate in (True, False)}
    everyone = list(range(refls))
    adds = None
    for at in range(len(pieces)):
        backs = middle(at, cross(sends[at]))
        returned = cross(backs)
        if at + 1 < len(pieces):
            adds, unused = y_adjoint(at, returned, jobs[True] + jobs[False], everyone, adds)

    for_mate, done = y_adjoint(at, returned, jobs[True], everyone[1:], adds)
    mine, unused = y_adjoint(at, returned, jobs[False], everyone[1:], adds, (done,))
    sums, others = [], [[] for _ in range(1, refls)]
    for part in range(splits):
        for k in range(1, refls):
            shape = (2 * portion * rows + (8 * planes if part == 0 else 0), depth)
            from_mate = swap(for_mate[jobs[True][part]][k], "slab", 1)
            (total,) = call(
                functools.partial(pack_kernel, part == 0),
                [shape],
                [place],
                (mine[jobs[False][part]][k], from_mate, *fields),
                [],
                4 * cells,
                "pack",
            )
            sums.append(total)
            others[k - 1].append(swap(total, "refl", k))
    for_mate, unused = y_adjoint(at, returned, jobs[True], everyone[:1], adds, sums)
    mine, unused = y_adjoint(at, returned, jobs[False], everyone[:1], adds, sums)
    mates = [swap(for_mate[job][0], "slab", 1) for job in jobs[True]]
    own = [mine[job][0] for job in jobs[False]]
    edges = call(edges_kernel, [(4, rows, depth)] * 2, [place], fields, [], cells, "edges", first=sums)
    halos = (swap(edges[0], "slab", 1), swap_outward(edges[1], "slab"), *[one[0] for one in others])
    (lapped,) = call(
        functools.partial(laplace_kernel, refls),
        [(4, planes, rows, depth)],
        [place],
        (*fields, *halos),
        [],
        30 * cells,
        "laplace",
    )
    result = ()
    for part in range(splits):
        result = call(
            functools.partial(final_kernel, refls),
            [(planes, rows, depth), (3, planes, rows, depth)],
            [place, *params],
            (
                amplitude,
                support,
                lapped,
                own[part],
                mates[part],
                *[one[part] for one in others],
                *[made[part][k][0] for k in range(refls)],
            ),
            [],
            20 * refls * cells // splits,
            "final",
            {
                0: ((portion, rows, depth), (part, 0, 0)),
                1: ((portion, rows * refls, depth), (part, 0, 0)),
                2: ((4, portion, rows, depth), (0, part, 0, 0)),
            },
            out_blocks=[((portion, rows, depth), (part, 0, 0)), ((3, portion, rows, depth), (0, part, 0, 0))],
            carried=result,
        )
    return tuple(result)


def solution(mesh):
    placed = (
        P("slab", "refl", None),
        P(None, "slab", "refl", None),
        P("slab", None, None),
        P("refl", None),
        P("refl"),
        P("refl", None, "slab", None),
    )
    return jax.shard_map(
        body,
        mesh=mesh,
        in_specs=placed,
        out_specs=(P("slab", "refl", None), P(None, "slab", "refl", None)),
        check_vma=False,
    )
```

```python
import functools

import jax
import jax.numpy as jnp
import ml_dtypes
import numpy as np
from jax import lax
from jax.experimental import pallas as pl
from jax.experimental.pallas import tpu as pltpu
from jax.sharding import PartitionSpec as P

STRAIN_WEIGHT = 0.05
EDGE_WEIGHT = 0.05
PIECES = (8, 8)
F32 = jnp.float32
BF16 = jnp.bfloat16


def split_table(table):
    high = table.astype(ml_dtypes.bfloat16)
    low = (table - high.astype(np.float64)).astype(ml_dtypes.bfloat16)
    return high, low


def forward_table(freqs, places, length):
    angle = 2.0 * np.pi / length * (freqs[:, None] * places[None, :] % length)
    cosine = np.cos(angle) * length ** (-0.5)
    sine = np.sin(angle) * length ** (-0.5)
    return np.block([[cosine, sine], [-sine, cosine]])


def turn_fits():
    nodes = np.cos(np.pi * (np.arange(400) + 0.5) / 400)
    t = (nodes + 1.0) / 8.0
    r = np.sqrt(t)
    fits = []
    for values, degree in ((np.cos(2 * np.pi * r), 8), (np.sin(2 * np.pi * r) / r, 8)):
        cheb = np.polynomial.chebyshev.Chebyshev.fit(t, values, degree, domain=[0.0, 0.25])
        fits.append([float(c) for c in cheb.convert(kind=np.polynomial.Polynomial).coef])
    return fits


COS_FIT, SIN_FIT = turn_fits()


def series(coefs, t):
    total = jnp.full_like(t, coefs[-1])
    for coef in coefs[-2::-1]:
        total = total * t + coef
    return total


def halves(x):
    high = x.astype(BF16)
    return high, (x - high.astype(F32)).astype(BF16)


def dot(a, b):
    return jnp.dot(a, b, preferred_element_type=F32)


def dot_pairs(a, b):
    return dot(a[0], b[0]) + (dot(a[0], b[1]) + dot(a[1], b[0]))


SMEM = pl.BlockSpec(memory_space=pltpu.SMEM)


def whole(shape):
    return pl.BlockSpec(tuple(shape), lambda step, rank=len(shape): (0,) * rank)


def call(kernel, outs, scalars, operands, scratch, flops, name, blocks=None, first=(), vmem=48, out_blocks=None, carried=()):
    blocks = blocks or {}
    inputs = len(scalars) + len(operands)
    specs = [SMEM] * len(scalars)
    moved = 4 * sum(int(np.prod(shape)) for shape in outs)
    for at, operand in enumerate(operands):
        if at in blocks and blocks[at] is None:
            shape = (0,)
            specs.append(pl.BlockSpec(memory_space=pl.ANY))
        elif at in blocks:
            shape, index = blocks[at]
            specs.append(pl.BlockSpec(shape, lambda step, index=index: index))
        else:
            shape = operand.shape
            specs.append(whole(shape))
        moved += int(np.prod(shape)) * operand.dtype.itemsize
    first = (*first, *carried)
    specs += [pl.BlockSpec(memory_space=pl.ANY)] * len(first)
    aliases = {len(specs) - len(carried) + i: i for i in range(len(carried))}

    def run(*refs):
        kernel(*refs[:inputs], *refs[inputs + len(first) :])

    return pl.pallas_call(
        run,
        grid=(1,),
        out_shape=[jax.ShapeDtypeStruct(shape, F32) for shape in outs],
        in_specs=specs,
        out_specs=[
            pl.BlockSpec(shape, lambda step, index=index: index)
            for shape, index in out_blocks or [(shape, (0,) * len(shape)) for shape in outs]
        ],
        input_output_aliases=aliases,
        scratch_shapes=scratch,
        compiler_params=pltpu.CompilerParams(vmem_limit_bytes=vmem * 1024 * 1024),
        cost_estimate=pl.CostEstimate(flops=int(flops), bytes_accessed=int(moved), transcendentals=0),
        name=name,
    )(*scalars, *operands, *first)


def field_of(place, amp, disp, sup, f, p):
    if f > 0:
        return disp[f - 1, p]
    rows = amp.shape[1]
    return sup[p, pl.ds(pl.multiple_of(place[2] * rows, rows), rows), :].astype(F32) * amp[p]


def edges_kernel(place, amp, disp, sup, x_mate, x_out):
    planes = amp.shape[0]
    core = place[1]
    for f in range(4):
        x_mate[f] = field_of(place, amp, disp, sup, f, (1 - core) * (planes - 1))
        x_out[f] = field_of(place, amp, disp, sup, f, core * (planes - 1))


def pack_kernel(edged, place, a, b, amp, disp, sup, out):
    portion, rows, depth = a.shape[1:]
    planes = amp.shape[0]
    for c in range(2):
        for p in range(portion):
            at = (c * portion + p) * rows
            out[at : at + rows, :] = a[c, p] + b[c, p]
    if edged:
        for f in range(4):
            for p in range(planes):
                value = field_of(place, amp, disp, sup, f, p)
                at = 2 * portion * rows + f * planes + p
                out[at : at + 1, :] = value[:1]
                at += 4 * planes
                out[at : at + 1, :] = value[rows - 1 :]


def laplace_kernel(refls, place, amp, disp, sup, x_mate, x_out, *refs):
    planes, rows, depth = amp.shape
    packs, out = refs[:-1], refs[-1]
    refl = place[2]
    low_core = place[1] == 0
    row = lax.broadcasted_iota(jnp.int32, (rows, depth), 0)
    lane = lax.broadcasted_iota(jnp.int32, (rows, depth), 1)
    for f in range(4):
        for p in range(planes):
            centre = field_of(place, amp, disp, sup, f, p)
            before, behind = jnp.zeros((1, depth), F32), jnp.zeros((1, depth), F32)
            for k in range(1, refls):
                at = packs[k - 1].shape[0] - 8 * planes + f * planes + p
                behind = jnp.where((refl ^ k) - refl == 1, packs[k - 1][at : at + 1, :], behind)
                at += 4 * planes
                before = jnp.where(refl - (refl ^ k) == 1, packs[k - 1][at : at + 1, :], before)
            if p == 0:
                beside = jnp.where(low_core, x_out[f], x_mate[f])
            else:
                beside = field_of(place, amp, disp, sup, f, p - 1)
            if p == planes - 1:
                beside = beside + jnp.where(low_core, x_mate[f], x_out[f])
            else:
                beside = beside + field_of(place, amp, disp, sup, f, p + 1)
            beside = beside + jnp.where(row == 0, before, pltpu.roll(centre, 1, 0))
            beside = beside + jnp.where(row == rows - 1, behind, pltpu.roll(centre, rows - 1, 0))
            beside = beside + jnp.where(lane == 0, 0.0, pltpu.roll(centre, 1, 1))
            beside = beside + jnp.where(lane == depth - 1, 0.0, pltpu.roll(centre, depth - 1, 1))
            out[f, p] = 6.0 * centre - beside


def object_kernel(which, grid, place, *refs):
    params, (amp, disp, sup), outs = refs[: len(which)], refs[len(which) : len(which) + 3], refs[len(which) + 3 :]
    planes, rows, depth = amp.shape
    first = pl.multiple_of(place[2] * rows, rows)
    zed = lax.broadcasted_iota(jnp.int32, (rows, depth), 1).astype(F32) * (1.0 / grid)

    def plane(p, carry):
        weight = sup[p, pl.ds(first, rows), :].astype(F32) * amp[p]
        parts = [disp[0, p], disp[1, p], disp[2, p]]
        for at, param in enumerate(params):
            phase = param[0] * parts[0] + param[1] * parts[1] + param[2] * parts[2]
            shifted = param[3] * zed
            turns = phase * (0.5 / np.pi) + (shifted - jnp.floor(shifted))
            turns = turns - jnp.floor(turns + 0.5)
            square = turns * turns
            cosine = series(COS_FIT, square)
            sine = series(SIN_FIT, square) * turns
            outs[2 * at][0, p] = cosine
            outs[2 * at][1, p] = sine
            outs[2 * at + 1][0, p] = weight * cosine
            outs[2 * at + 1][1, p] = weight * sine
        return carry

    lax.fori_loop(0, planes, plane, 0)


def y_forward_kernel(refls, chips, splits, targets, place, *refs):
    count = 2 * refls * splits
    parts, tables, outs = refs[:count], refs[count], refs[count + 1 : -2]
    hold_high, hold_low = refs[-2:]
    chip, core, refl = place[0], place[1], place[2]
    portion, rows, depth = parts[0].shape[1:]
    planes = portion * splits
    length = rows * refls
    share = tables.shape[2] // chips

    def order(which):
        return jnp.concatenate(
            [tables[core, which, pl.ds(pl.multiple_of((chip ^ k) * share, share), share), :] for k in targets],
            axis=0,
        )

    table = (order(0), order(1))
    for src in range(2):
        for p in range(planes):
            lane = (src * planes + p) * depth
            for c in range(2):
                for k in range(refls):
                    part = parts[(src * refls + k) * splits + p // portion]
                    one, two = halves(part[c, p % portion])
                    at = pl.ds(pl.multiple_of(c * length + (refl ^ k) * rows, rows), rows)
                    hold_high[at, lane : lane + depth] = one
                    hold_low[at, lane : lane + depth] = two
    for src in range(2):
        for p in range(0, planes, 2):
            lane = (src * planes + p) * depth
            operand = (hold_high[:, lane : lane + 2 * depth], hold_low[:, lane : lane + 2 * depth])
            result = dot_pairs(table, operand)
            base = (core if src == 0 else 1 - core) * planes + p
            for i in range(len(targets)):
                for j in range(2):
                    outs[i][base + j] = result[i * share : (i + 1) * share, j * depth : (j + 1) * depth]


def middle_kernel(chips, first, place, *refs):
    got, intensity = refs[:chips], refs[chips]
    fwd = (refs[chips + 1][...], refs[chips + 2][...])
    bwd = (refs[chips + 3][...], refs[chips + 4][...])
    outs = refs[chips + 5 : -4]
    gather, scatter, measured, arrived = refs[-4:]
    chip = place[0]
    group, width, depth = got[0].shape
    rows = width // 2
    edge = group * chips
    grid = 2 * edge
    batch = gather.shape[1] // depth
    held = first // 8 * 8
    load = pltpu.make_async_copy(intensity.at[0, :, held : held + measured.shape[1], :], measured, arrived)
    load.start()

    def place_of(c, k):
        return pl.ds(pl.multiple_of(c * edge + (chip ^ k) * group, group), group)

    for key in range(0, rows, batch):
        for k in range(chips):
            for c in range(2):
                for j in range(batch):
                    gather[place_of(c, k), j * depth : (j + 1) * depth] = got[k][:, (key + j) * 2 + c, :]
        one = dot_pairs(fwd, halves(gather[...]))
        if key == 0:
            load.wait()
        back = []
        for j in range(batch):
            lines = [one[c * grid : (c + 1) * grid, j * depth : (j + 1) * depth] for c in range(2)]
            spectrum = dot_pairs(halves(jnp.concatenate(lines, axis=1)), bwd)
            real, imag = spectrum[:, :grid], spectrum[:, grid:]
            excess = 4.0 * (real * real + imag * imag - measured[:, first - held + key + j, :])
            back.append(dot_pairs(halves(jnp.concatenate([excess * real, excess * imag], axis=1)), fwd))
        lines = [jnp.concatenate([b[:, c * depth : (c + 1) * depth] for b in back], axis=1) for c in range(2)]
        scatter[...] = dot_pairs(bwd, halves(jnp.concatenate(lines, axis=0)))
        for k in range(chips):
            for c in range(2):
                for j in range(batch):
                    outs[k][:, (key + j) * 2 + c, :] = scatter[place_of(c, k), j * depth : (j + 1) * depth]


def y_adjoint_kernel(chips, jobs, parts, place, *refs):
    got, tables = refs[:chips], refs[chips]
    total = len(parts) * len(jobs)
    adds, outs = refs[chips + 1 : -2 - total], refs[-2 - total : -2]
    done, hold = refs[-2:]
    done[...] = jnp.zeros_like(done)
    chip, core, refl = place[0], place[1], place[2]
    planes, rows, depth = outs[0].shape[1:]
    width = got[0].shape[1]

    def order(which):
        pieces = []
        for q in parts:
            for c in range(2):
                at = pl.multiple_of(((refl ^ q) * 2 + c) * rows, rows)
                pieces.append(tables[core, which, pl.ds(at, rows), :])
        return jnp.concatenate(pieces, axis=0)

    table = (order(0), order(1))
    for job, (mate, first) in enumerate(jobs):
        base = (1 - core if mate else core) * (got[0].shape[0] // 2) + first
        for p in range(planes):
            lane = (job * planes + p) * depth
            for k in range(chips):
                at = pl.ds(pl.multiple_of((chip ^ k) * width, width), width)
                hold[at, lane : lane + depth] = got[k][base + p]
    for job in range(len(jobs)):
        for p in range(0, planes, 2):
            lane = (job * planes + p) * depth
            result = dot_pairs(table, halves(hold[:, lane : lane + 2 * depth]))
            for i in range(len(parts)):
                for c in range(2):
                    at = (i * 2 + c) * rows
                    for j in range(2):
                        value = result[at : at + rows, j * depth : (j + 1) * depth]
                        if adds:
                            value = value + adds[job * len(parts) + i][c, p + j]
                        outs[job * len(parts) + i][c, p + j] = value


def final_kernel(refls, place, *refs):
    params = refs[:refls]
    amp, sup, lapped, own, mate = refs[refls : refls + 5]
    others, phases = refs[refls + 5 : 2 * refls + 4], refs[2 * refls + 4 : -2]
    out_amp, out_disp = refs[-2:]
    planes, rows, depth = amp.shape
    first = pl.multiple_of(place[2] * rows, rows)

    def plane(p, carry):
        mask = sup[p, pl.ds(first, rows), :].astype(F32)
        weight = mask * amp[p]
        total = jnp.zeros((rows, depth), F32)
        moved = [jnp.zeros((rows, depth), F32) for _ in range(3)]
        for k in range(refls):
            if k == 0:
                real, imag = [own[c, p] + mate[c, p] for c in range(2)]
            else:
                at = [pl.ds(pl.multiple_of((c * planes + p) * rows, rows), rows) for c in range(2)]
                real, imag = [others[k - 1][at[c], :] for c in range(2)]
            cosine, sine = phases[k][0, p], phases[k][1, p]
            total = total + (real * cosine + imag * sine)
            across = weight * (imag * cosine - real * sine)
            moved = [m + params[k][c] * across for c, m in enumerate(moved)]
        out_amp[p] = mask * total + (2.0 * EDGE_WEIGHT) * (mask * lapped[0, p])
        for c in range(3):
            out_disp[c, p] = moved[c] + (2.0 * STRAIN_WEIGHT) * lapped[c + 1, p]
        return carry

    lax.fori_loop(0, planes, plane, 0)


def swap(x, axis, bits):
    count = lax.axis_size(axis)
    return lax.ppermute(x, axis, [(i, i ^ bits) for i in range(count)])


def swap_outward(x, axis):
    count = lax.axis_size(axis)
    return lax.ppermute(x, axis, [pair for i in range(1, count - 1, 2) for pair in ((i, i + 1), (i + 1, i))])


def body(amplitude, displacement, support, miller, shift_kz, intensity):
    refls = lax.axis_size("refl")
    slabs = lax.axis_size("slab")
    chips = slabs // 2
    planes, rows, depth = amplitude.shape
    edge = planes * slabs
    grid = 2 * edge
    keys = grid // slabs
    pieces = PIECES if sum(PIECES) == keys else (keys,)
    splits = 2 if planes % 8 == 0 else 1
    portion = planes // splits
    group = 2 * planes
    refl = lax.axis_index("refl")
    slab = lax.axis_index("slab")
    place = jnp.stack([slab // 2, slab % 2, refl]).astype(jnp.int32)
    cells = planes * rows * depth
    part_shape = (2, portion, rows, depth)

    every, inner = np.arange(grid), np.arange(edge)
    table = forward_table(every, inner, grid)
    constants = [jnp.asarray(t) for one in (table, table.T) for t in split_table(one)]
    by_key = table.reshape(2, chips, 2, keys, 2 * edge).transpose(2, 1, 3, 0, 4)

    def y_tables(at):
        first, count = sum(pieces[:at]), pieces[at]
        some = by_key[:, :, first : first + count].reshape(2, chips * count * 2, 2 * edge)
        fwd = jnp.asarray(np.stack(split_table(some), axis=1))
        some = some.reshape(2, chips * count * 2, 2, refls, rows)
        some = some.transpose(0, 3, 2, 4, 1).reshape(2, 2 * edge, chips * count * 2)
        return fwd, jnp.asarray(np.stack(split_table(some), axis=1))

    own_params = jnp.concatenate([miller[0].astype(F32), shift_kz.astype(F32)])
    fields = (amplitude, displacement, support)
    def part_blocks(part, start=0):
        return {
            start: ((portion, rows, depth), (part, 0, 0)),
            start + 1: ((3, portion, rows, depth), (0, part, 0, 0)),
            start + 2: ((portion, rows * refls, depth), (part, 0, 0)),
        }

    def make(part, which, vmem=48, first=()):
        made = call(
            functools.partial(object_kernel, which, grid),
            [part_shape] * (2 * len(which)),
            [place, *[params[k] for k in which]],
            fields,
            [],
            50 * len(which) * cells // splits,
            "object",
            part_blocks(part),
            first,
            vmem,
        )
        return {k: made[2 * i : 2 * i + 2] for i, k in enumerate(which)}

    params = [own_params] + [swap(own_params, "refl", k) for k in range(1, refls)]
    made = [make(0, list(range(1, refls)), 60)]
    made += [make(part, list(range(1, refls)), 60, [made[0][1][1]]) for part in range(1, splits)]
    held = [swap(made[part][k][1], "refl", k) for k in range(1, refls) for part in range(splits)]
    for part in range(splits):
        made[part].update(make(part, [0]))
    own_parts = [made[part][0][1] for part in range(splits)]
    own_mates = [swap(x, "slab", 1) for x in own_parts]
    mates = [swap(x, "slab", 1) for x in held]

    def y_forward(at, targets, first=()):
        made = call(
            functools.partial(y_forward_kernel, refls, chips, splits, targets),
            [(group, 2 * pieces[at], depth)] * len(targets),
            [place],
            (*own_parts, *held, *own_mates, *mates, y_tables(at)[0]),
            [pltpu.VMEM((2 * edge, group * depth), BF16)] * 2,
            6 * group * depth * 2 * edge * len(targets) * pieces[at] * 2,
            "y_forward",
            first=first,
        )
        return dict(zip(targets, made))

    def middle(at, got):
        first, count = sum(pieces[:at]), pieces[at]
        held = -(-(first + count) // 8) * 8 - first // 8 * 8
        return call(
            functools.partial(middle_kernel, chips, first),
            [(group, 2 * count, depth)] * chips,
            [place],
            (*got, intensity, *constants),
            [pltpu.VMEM((2 * edge, (count if count < 8 else count // 2 if count > 8 else 8) * depth), F32)] * 2
            + [pltpu.VMEM((grid, held, grid), F32), pltpu.SemaphoreType.DMA],
            6 * count * (2 * edge * 2 * grid * depth * 2 + grid * 2 * depth * 2 * grid * 2),
            "middle",
            {chips: None},
        )

    def y_adjoint(at, got, jobs, parts, adds=None, first=()):
        count = pieces[at]
        made = call(
            functools.partial(y_adjoint_kernel, chips, jobs, parts),
            [part_shape] * (len(parts) * len(jobs)) + [(8, 128)],
            [place],
            (*got, y_tables(at)[1], *([adds[job][k] for job in jobs for k in parts] if adds else [])),
            [pltpu.VMEM((chips * 2 * count, len(jobs) * portion * depth), F32)],
            6 * len(jobs) * portion * depth * len(parts) * 2 * rows * chips * 2 * count,
            "y_adjoint",
            first=first,
        )
        each = len(parts)
        return {job: dict(zip(parts, made[i * each : (i + 1) * each])) for i, job in enumerate(jobs)}, made[-1]

    def cross(sends):
        return [sends[0]] + [swap(sends[k], "slab", 2 * k) for k in range(1, chips)]

    arrived, first = [], ()
    for at in range(len(pieces)):
        arrived.append(cross(y_forward(at, list(range(chips)), first)))
        first = [arrived[at][chips // 2]]
    jobs = {mate: [(mate, part * portion) for part in range(splits)] for mate in (True, False)}
    everyone = list(range(refls))
    adds = None
    for at in range(len(pieces)):
        backs = middle(at, arrived[at])
        returned = cross(backs)
        if at + 1 < len(pieces):
            adds, unused = y_adjoint(at, returned, jobs[True] + jobs[False], everyone, adds)

    for_mate, done = y_adjoint(at, returned, jobs[True], everyone[1:], adds)
    mine, unused = y_adjoint(at, returned, jobs[False], everyone[1:], adds, (done,))
    sums, others = [], [[] for _ in range(1, refls)]
    for part in range(splits):
        for k in range(1, refls):
            shape = (2 * portion * rows + (8 * planes if part == 0 else 0), depth)
            from_mate = swap(for_mate[jobs[True][part]][k], "slab", 1)
            (total,) = call(
                functools.partial(pack_kernel, part == 0),
                [shape],
                [place],
                (mine[jobs[False][part]][k], from_mate, *fields),
                [],
                4 * cells,
                "pack",
            )
            sums.append(total)
            others[k - 1].append(swap(total, "refl", k))
    for_mate, unused = y_adjoint(at, returned, jobs[True], everyone[:1], adds, sums)
    mine, unused = y_adjoint(at, returned, jobs[False], everyone[:1], adds, sums)
    mates = [swap(for_mate[job][0], "slab", 1) for job in jobs[True]]
    own = [mine[job][0] for job in jobs[False]]
    edges = call(edges_kernel, [(4, rows, depth)] * 2, [place], fields, [], cells, "edges", first=sums)
    halos = (swap(edges[0], "slab", 1), swap_outward(edges[1], "slab"), *[one[0] for one in others])
    (lapped,) = call(
        functools.partial(laplace_kernel, refls),
        [(4, planes, rows, depth)],
        [place],
        (*fields, *halos),
        [],
        30 * cells,
        "laplace",
    )
    result = ()
    for part in range(splits):
        result = call(
            functools.partial(final_kernel, refls),
            [(planes, rows, depth), (3, planes, rows, depth)],
            [place, *params],
            (
                amplitude,
                support,
                lapped,
                own[part],
                mates[part],
                *[one[part] for one in others],
                *[made[part][k][0] for k in range(refls)],
            ),
            [],
            20 * refls * cells // splits,
            "final",
            {
                0: ((portion, rows, depth), (part, 0, 0)),
                1: ((portion, rows * refls, depth), (part, 0, 0)),
                2: ((4, portion, rows, depth), (0, part, 0, 0)),
            },
            out_blocks=[((portion, rows, depth), (part, 0, 0)), ((3, portion, rows, depth), (0, part, 0, 0))],
            carried=result,
        )
    return tuple(result)


def solution(mesh):
    placed = (
        P("slab", "refl", None),
        P(None, "slab", "refl", None),
        P("slab", None, None),
        P("refl", None),
        P("refl"),
        P("refl", None, "slab", None),
    )
    return jax.shard_map(
        body,
        mesh=mesh,
        in_specs=placed,
        out_specs=(P("slab", "refl", None), P(None, "slab", "refl", None)),
        check_vma=False,
    )
```

```python
import functools

import jax
import jax.numpy as jnp
import ml_dtypes
import numpy as np
from jax import lax
from jax.experimental import pallas as pl
from jax.experimental.pallas import tpu as pltpu
from jax.sharding import PartitionSpec as P

STRAIN_WEIGHT = 0.05
EDGE_WEIGHT = 0.05
PIECES = (8, 8)
F32 = jnp.float32
BF16 = jnp.bfloat16


def split_table(table):
    high = table.astype(ml_dtypes.bfloat16)
    low = (table - high.astype(np.float64)).astype(ml_dtypes.bfloat16)
    return high, low


def forward_table(freqs, places, length):
    angle = 2.0 * np.pi / length * (freqs[:, None] * places[None, :] % length)
    cosine = np.cos(angle) * length ** (-0.5)
    sine = np.sin(angle) * length ** (-0.5)
    return np.block([[cosine, sine], [-sine, cosine]])


def turn_fits():
    nodes = np.cos(np.pi * (np.arange(400) + 0.5) / 400)
    t = (nodes + 1.0) / 8.0
    r = np.sqrt(t)
    fits = []
    for values, degree in ((np.cos(2 * np.pi * r), 8), (np.sin(2 * np.pi * r) / r, 8)):
        cheb = np.polynomial.chebyshev.Chebyshev.fit(t, values, degree, domain=[0.0, 0.25])
        fits.append([float(c) for c in cheb.convert(kind=np.polynomial.Polynomial).coef])
    return fits


COS_FIT, SIN_FIT = turn_fits()


def series(coefs, t):
    total = jnp.full_like(t, coefs[-1])
    for coef in coefs[-2::-1]:
        total = total * t + coef
    return total


def halves(x):
    high = x.astype(BF16)
    return high, (x - high.astype(F32)).astype(BF16)


def dot(a, b):
    return jnp.dot(a, b, preferred_element_type=F32)


def dot_pairs(a, b):
    return dot(a[0], b[0]) + (dot(a[0], b[1]) + dot(a[1], b[0]))


SMEM = pl.BlockSpec(memory_space=pltpu.SMEM)


def whole(shape):
    return pl.BlockSpec(tuple(shape), lambda step, rank=len(shape): (0,) * rank)


def call(kernel, outs, scalars, operands, scratch, flops, name, blocks=None, first=(), vmem=48, out_blocks=None, carried=()):
    blocks = blocks or {}
    inputs = len(scalars) + len(operands)
    specs = [SMEM] * len(scalars)
    moved = 4 * sum(int(np.prod(shape)) for shape in outs)
    for at, operand in enumerate(operands):
        if at in blocks and blocks[at] is None:
            shape = (0,)
            specs.append(pl.BlockSpec(memory_space=pl.ANY))
        elif at in blocks:
            shape, index = blocks[at]
            specs.append(pl.BlockSpec(shape, lambda step, index=index: index))
        else:
            shape = operand.shape
            specs.append(whole(shape))
        moved += int(np.prod(shape)) * operand.dtype.itemsize
    first = (*first, *carried)
    specs += [pl.BlockSpec(memory_space=pl.ANY)] * len(first)
    aliases = {len(specs) - len(carried) + i: i for i in range(len(carried))}

    def run(*refs):
        kernel(*refs[:inputs], *refs[inputs + len(first) :])

    return pl.pallas_call(
        run,
        grid=(1,),
        out_shape=[jax.ShapeDtypeStruct(shape, F32) for shape in outs],
        in_specs=specs,
        out_specs=[
            pl.BlockSpec(shape, lambda step, index=index: index)
            for shape, index in out_blocks or [(shape, (0,) * len(shape)) for shape in outs]
        ],
        input_output_aliases=aliases,
        scratch_shapes=scratch,
        compiler_params=pltpu.CompilerParams(vmem_limit_bytes=vmem * 1024 * 1024),
        cost_estimate=pl.CostEstimate(flops=int(flops), bytes_accessed=int(moved), transcendentals=0),
        name=name,
    )(*scalars, *operands, *first)


def field_of(place, amp, disp, sup, f, p):
    if f > 0:
        return disp[f - 1, p]
    rows = amp.shape[1]
    return sup[p, pl.ds(pl.multiple_of(place[2] * rows, rows), rows), :].astype(F32) * amp[p]


def edges_kernel(place, amp, disp, sup, x_mate, x_out):
    planes = amp.shape[0]
    core = place[1]
    for f in range(4):
        x_mate[f] = field_of(place, amp, disp, sup, f, (1 - core) * (planes - 1))
        x_out[f] = field_of(place, amp, disp, sup, f, core * (planes - 1))


def pack_kernel(edged, place, a, b, amp, disp, sup, out):
    portion, rows, depth = a.shape[1:]
    planes = amp.shape[0]
    for c in range(2):
        for p in range(portion):
            at = (c * portion + p) * rows
            out[at : at + rows, :] = a[c, p] + b[c, p]
    if edged:
        for f in range(4):
            for p in range(planes):
                value = field_of(place, amp, disp, sup, f, p)
                at = 2 * portion * rows + f * planes + p
                out[at : at + 1, :] = value[:1]
                at += 4 * planes
                out[at : at + 1, :] = value[rows - 1 :]


def laplace_kernel(refls, place, amp, disp, sup, x_mate, x_out, *refs):
    planes, rows, depth = amp.shape
    packs, out = refs[:-1], refs[-1]
    refl = place[2]
    low_core = place[1] == 0
    row = lax.broadcasted_iota(jnp.int32, (rows, depth), 0)
    lane = lax.broadcasted_iota(jnp.int32, (rows, depth), 1)
    for f in range(4):
        for p in range(planes):
            centre = field_of(place, amp, disp, sup, f, p)
            before, behind = jnp.zeros((1, depth), F32), jnp.zeros((1, depth), F32)
            for k in range(1, refls):
                at = packs[k - 1].shape[0] - 8 * planes + f * planes + p
                behind = jnp.where((refl ^ k) - refl == 1, packs[k - 1][at : at + 1, :], behind)
                at += 4 * planes
                before = jnp.where(refl - (refl ^ k) == 1, packs[k - 1][at : at + 1, :], before)
            if p == 0:
                beside = jnp.where(low_core, x_out[f], x_mate[f])
            else:
                beside = field_of(place, amp, disp, sup, f, p - 1)
            if p == planes - 1:
                beside = beside + jnp.where(low_core, x_mate[f], x_out[f])
            else:
                beside = beside + field_of(place, amp, disp, sup, f, p + 1)
            beside = beside + jnp.where(row == 0, before, pltpu.roll(centre, 1, 0))
            beside = beside + jnp.where(row == rows - 1, behind, pltpu.roll(centre, rows - 1, 0))
            beside = beside + jnp.where(lane == 0, 0.0, pltpu.roll(centre, 1, 1))
            beside = beside + jnp.where(lane == depth - 1, 0.0, pltpu.roll(centre, depth - 1, 1))
            out[f, p] = 6.0 * centre - beside


def object_kernel(which, grid, place, *refs):
    params, (amp, disp, sup), outs = refs[: len(which)], refs[len(which) : len(which) + 3], refs[len(which) + 3 :]
    planes, rows, depth = amp.shape
    first = pl.multiple_of(place[2] * rows, rows)
    zed = lax.broadcasted_iota(jnp.int32, (rows, depth), 1).astype(F32) * (1.0 / grid)

    def plane(p, carry):
        weight = sup[p, pl.ds(first, rows), :].astype(F32) * amp[p]
        parts = [disp[0, p], disp[1, p], disp[2, p]]
        for at, param in enumerate(params):
            phase = param[0] * parts[0] + param[1] * parts[1] + param[2] * parts[2]
            shifted = param[3] * zed
            turns = phase * (0.5 / np.pi) + (shifted - jnp.floor(shifted))
            turns = turns - jnp.floor(turns + 0.5)
            square = turns * turns
            cosine = series(COS_FIT, square)
            sine = series(SIN_FIT, square) * turns
            outs[2 * at][0, p] = cosine
            outs[2 * at][1, p] = sine
            outs[2 * at + 1][0, p] = weight * cosine
            outs[2 * at + 1][1, p] = weight * sine
        return carry

    lax.fori_loop(0, planes, plane, 0)


def y_forward_kernel(refls, chips, splits, targets, place, *refs):
    count = 2 * refls * splits
    parts, tables, outs = refs[:count], refs[count], refs[count + 1 : -2]
    hold_high, hold_low = refs[-2:]
    chip, core, refl = place[0], place[1], place[2]
    portion, rows, depth = parts[0].shape[1:]
    planes = portion * splits
    length = rows * refls
    share = tables.shape[2] // chips

    def order(which):
        return jnp.concatenate(
            [tables[core, which, pl.ds(pl.multiple_of((chip ^ k) * share, share), share), :] for k in targets],
            axis=0,
        )

    table = (order(0), order(1))
    for src in range(2):
        for p in range(planes):
            lane = (src * planes + p) * depth
            for c in range(2):
                for k in range(refls):
                    part = parts[(src * refls + k) * splits + p // portion]
                    one, two = halves(part[c, p % portion])
                    at = pl.ds(pl.multiple_of(c * length + (refl ^ k) * rows, rows), rows)
                    hold_high[at, lane : lane + depth] = one
                    hold_low[at, lane : lane + depth] = two
    for src in range(2):
        for p in range(0, planes, 2):
            lane = (src * planes + p) * depth
            operand = (hold_high[:, lane : lane + 2 * depth], hold_low[:, lane : lane + 2 * depth])
            result = dot_pairs(table, operand)
            base = (core if src == 0 else 1 - core) * planes + p
            for i in range(len(targets)):
                for j in range(2):
                    outs[i][base + j] = result[i * share : (i + 1) * share, j * depth : (j + 1) * depth]


def middle_kernel(chips, first, place, *refs):
    got, intensity = refs[:chips], refs[chips]
    fwd = (refs[chips + 1][...], refs[chips + 2][...])
    bwd = (refs[chips + 3][...], refs[chips + 4][...])
    outs = refs[chips + 5 : -4]
    gather, scatter, measured, arrived = refs[-4:]
    chip = place[0]
    group, width, depth = got[0].shape
    rows = width // 2
    edge = group * chips
    grid = 2 * edge
    batch = gather.shape[1] // depth
    held = first // 8 * 8
    load = pltpu.make_async_copy(intensity.at[0, :, held : held + measured.shape[1], :], measured, arrived)
    load.start()

    def place_of(c, k):
        return pl.ds(pl.multiple_of(c * edge + (chip ^ k) * group, group), group)

    for key in range(0, rows, batch):
        for k in range(chips):
            for c in range(2):
                for j in range(batch):
                    gather[place_of(c, k), j * depth : (j + 1) * depth] = got[k][:, (key + j) * 2 + c, :]
        one = dot_pairs(fwd, halves(gather[...]))
        if key == 0:
            load.wait()
        back = []
        for j in range(batch):
            lines = [one[c * grid : (c + 1) * grid, j * depth : (j + 1) * depth] for c in range(2)]
            spectrum = dot_pairs(halves(jnp.concatenate(lines, axis=1)), bwd)
            real, imag = spectrum[:, :grid], spectrum[:, grid:]
            excess = 4.0 * (real * real + imag * imag - measured[:, first - held + key + j, :])
            back.append(dot_pairs(halves(jnp.concatenate([excess * real, excess * imag], axis=1)), fwd))
        lines = [jnp.concatenate([b[:, c * depth : (c + 1) * depth] for b in back], axis=1) for c in range(2)]
        scatter[...] = dot_pairs(bwd, halves(jnp.concatenate(lines, axis=0)))
        for k in range(chips):
            for c in range(2):
                for j in range(batch):
                    outs[k][:, (key + j) * 2 + c, :] = scatter[place_of(c, k), j * depth : (j + 1) * depth]


def y_adjoint_kernel(chips, jobs, parts, place, *refs):
    got, tables = refs[:chips], refs[chips]
    total = len(parts) * len(jobs)
    adds, outs = refs[chips + 1 : -2 - total], refs[-2 - total : -2]
    done, hold = refs[-2:]
    done[...] = jnp.zeros_like(done)
    chip, core, refl = place[0], place[1], place[2]
    planes, rows, depth = outs[0].shape[1:]
    width = got[0].shape[1]

    def order(which):
        pieces = []
        for q in parts:
            for c in range(2):
                at = pl.multiple_of(((refl ^ q) * 2 + c) * rows, rows)
                pieces.append(tables[core, which, pl.ds(at, rows), :])
        return jnp.concatenate(pieces, axis=0)

    table = (order(0), order(1))
    for job, (mate, first) in enumerate(jobs):
        base = (1 - core if mate else core) * (got[0].shape[0] // 2) + first
        for p in range(planes):
            lane = (job * planes + p) * depth
            for k in range(chips):
                at = pl.ds(pl.multiple_of((chip ^ k) * width, width), width)
                hold[at, lane : lane + depth] = got[k][base + p]
    for job in range(len(jobs)):
        for p in range(0, planes, 2):
            lane = (job * planes + p) * depth
            result = dot_pairs(table, halves(hold[:, lane : lane + 2 * depth]))
            for i in range(len(parts)):
                for c in range(2):
                    at = (i * 2 + c) * rows
                    for j in range(2):
                        value = result[at : at + rows, j * depth : (j + 1) * depth]
                        if adds:
                            value = value + adds[job * len(parts) + i][c, p + j]
                        outs[job * len(parts) + i][c, p + j] = value


def final_kernel(refls, place, *refs):
    params = refs[:refls]
    amp, sup, lapped, own, mate = refs[refls : refls + 5]
    others, phases = refs[refls + 5 : 2 * refls + 4], refs[2 * refls + 4 : -2]
    out_amp, out_disp = refs[-2:]
    planes, rows, depth = amp.shape
    first = pl.multiple_of(place[2] * rows, rows)

    def plane(p, carry):
        mask = sup[p, pl.ds(first, rows), :].astype(F32)
        weight = mask * amp[p]
        total = jnp.zeros((rows, depth), F32)
        moved = [jnp.zeros((rows, depth), F32) for _ in range(3)]
        for k in range(refls):
            if k == 0:
                real, imag = [own[c, p] + mate[c, p] for c in range(2)]
            else:
                at = [pl.ds(pl.multiple_of((c * planes + p) * rows, rows), rows) for c in range(2)]
                real, imag = [others[k - 1][at[c], :] for c in range(2)]
            cosine, sine = phases[k][0, p], phases[k][1, p]
            total = total + (real * cosine + imag * sine)
            across = weight * (imag * cosine - real * sine)
            moved = [m + params[k][c] * across for c, m in enumerate(moved)]
        out_amp[p] = mask * total + (2.0 * EDGE_WEIGHT) * (mask * lapped[0, p])
        for c in range(3):
            out_disp[c, p] = moved[c] + (2.0 * STRAIN_WEIGHT) * lapped[c + 1, p]
        return carry

    lax.fori_loop(0, planes, plane, 0)


def swap(x, axis, bits):
    count = lax.axis_size(axis)
    return lax.ppermute(x, axis, [(i, i ^ bits) for i in range(count)])


def swap_outward(x, axis):
    count = lax.axis_size(axis)
    return lax.ppermute(x, axis, [pair for i in range(1, count - 1, 2) for pair in ((i, i + 1), (i + 1, i))])


def body(amplitude, displacement, support, miller, shift_kz, intensity):
    refls = lax.axis_size("refl")
    slabs = lax.axis_size("slab")
    chips = slabs // 2
    planes, rows, depth = amplitude.shape
    edge = planes * slabs
    grid = 2 * edge
    keys = grid // slabs
    pieces = PIECES if sum(PIECES) == keys else (keys,)
    splits = 2 if planes % 8 == 0 else 1
    portion = planes // splits
    group = 2 * planes
    refl = lax.axis_index("refl")
    slab = lax.axis_index("slab")
    place = jnp.stack([slab // 2, slab % 2, refl]).astype(jnp.int32)
    cells = planes * rows * depth
    part_shape = (2, portion, rows, depth)

    every, inner = np.arange(grid), np.arange(edge)
    table = forward_table(every, inner, grid)
    constants = [jnp.asarray(t) for one in (table, table.T) for t in split_table(one)]
    by_key = table.reshape(2, chips, 2, keys, 2 * edge).transpose(2, 1, 3, 0, 4)

    def y_tables(at):
        first, count = sum(pieces[:at]), pieces[at]
        some = by_key[:, :, first : first + count].reshape(2, chips * count * 2, 2 * edge)
        fwd = jnp.asarray(np.stack(split_table(some), axis=1))
        some = some.reshape(2, chips * count * 2, 2, refls, rows)
        some = some.transpose(0, 3, 2, 4, 1).reshape(2, 2 * edge, chips * count * 2)
        return fwd, jnp.asarray(np.stack(split_table(some), axis=1))

    own_params = jnp.concatenate([miller[0].astype(F32), shift_kz.astype(F32)])
    fields = (amplitude, displacement, support)
    def part_blocks(part, start=0):
        return {
            start: ((portion, rows, depth), (part, 0, 0)),
            start + 1: ((3, portion, rows, depth), (0, part, 0, 0)),
            start + 2: ((portion, rows * refls, depth), (part, 0, 0)),
        }

    def make(part, which, vmem=48, first=()):
        made = call(
            functools.partial(object_kernel, which, grid),
            [part_shape] * (2 * len(which)),
            [place, *[params[k] for k in which]],
            fields,
            [],
            50 * len(which) * cells // splits,
            "object",
            part_blocks(part),
            first,
            vmem,
        )
        return {k: made[2 * i : 2 * i + 2] for i, k in enumerate(which)}

    params = [own_params] + [swap(own_params, "refl", k) for k in range(1, refls)]
    made = [make(0, list(range(1, refls)), 60)]
    made += [make(part, list(range(1, refls)), 60, [made[0][1][1]]) for part in range(1, splits)]
    held = [swap(made[part][k][1], "refl", k) for k in range(1, refls) for part in range(splits)]
    for part in range(splits):
        made[part].update(make(part, [0]))
    own_parts = [made[part][0][1] for part in range(splits)]
    own_mates = [swap(x, "slab", 1) for x in own_parts]
    mates = [swap(x, "slab", 1) for x in held]

    def y_forward(at, targets, first=()):
        made = call(
            functools.partial(y_forward_kernel, refls, chips, splits, targets),
            [(group, 2 * pieces[at], depth)] * len(targets),
            [place],
            (*own_parts, *held, *own_mates, *mates, y_tables(at)[0]),
            [pltpu.VMEM((2 * edge, group * depth), BF16)] * 2,
            6 * group * depth * 2 * edge * len(targets) * pieces[at] * 2,
            "y_forward",
            first=first,
        )
        return dict(zip(targets, made))

    def middle(at, got):
        first, count = sum(pieces[:at]), pieces[at]
        held = -(-(first + count) // 8) * 8 - first // 8 * 8
        return call(
            functools.partial(middle_kernel, chips, first),
            [(group, 2 * count, depth)] * chips,
            [place],
            (*got, intensity, *constants),
            [pltpu.VMEM((2 * edge, (count if count < 8 else count // 2 if count > 8 else 8) * depth), F32)] * 2
            + [pltpu.VMEM((grid, held, grid), F32), pltpu.SemaphoreType.DMA],
            6 * count * (2 * edge * 2 * grid * depth * 2 + grid * 2 * depth * 2 * grid * 2),
            "middle",
            {chips: None},
        )

    def y_adjoint(at, got, jobs, parts, adds=None, first=()):
        count = pieces[at]
        made = call(
            functools.partial(y_adjoint_kernel, chips, jobs, parts),
            [part_shape] * (len(parts) * len(jobs)) + [(8, 128)],
            [place],
            (*got, y_tables(at)[1], *([adds[job][k] for job in jobs for k in parts] if adds else [])),
            [pltpu.VMEM((chips * 2 * count, len(jobs) * portion * depth), F32)],
            6 * len(jobs) * portion * depth * len(parts) * 2 * rows * chips * 2 * count,
            "y_adjoint",
            first=first,
        )
        each = len(parts)
        return {job: dict(zip(parts, made[i * each : (i + 1) * each])) for i, job in enumerate(jobs)}, made[-1]

    def cross(sends):
        return [sends[0]] + [swap(sends[k], "slab", 2 * k) for k in range(1, chips)]

    arrived, first = [], ()
    for at in range(len(pieces)):
        arrived.append(cross(y_forward(at, list(range(chips)), first)))
        first = [arrived[at][chips // 2 + 1]]
    jobs = {mate: [(mate, part * portion) for part in range(splits)] for mate in (True, False)}
    everyone = list(range(refls))
    adds = None
    for at in range(len(pieces)):
        backs = middle(at, arrived[at])
        returned = cross(backs)
        if at + 1 < len(pieces):
            adds, unused = y_adjoint(at, returned, jobs[True] + jobs[False], everyone, adds)

    for_mate, done = y_adjoint(at, returned, jobs[True], everyone[1:], adds)
    mine, unused = y_adjoint(at, returned, jobs[False], everyone[1:], adds, (done,))
    sums, others = [], [[] for _ in range(1, refls)]
    for part in range(splits):
        for k in range(1, refls):
            shape = (2 * portion * rows + (8 * planes if part == 0 else 0), depth)
            from_mate = swap(for_mate[jobs[True][part]][k], "slab", 1)
            (total,) = call(
                functools.partial(pack_kernel, part == 0),
                [shape],
                [place],
                (mine[jobs[False][part]][k], from_mate, *fields),
                [],
                4 * cells,
                "pack",
            )
            sums.append(total)
            others[k - 1].append(swap(total, "refl", k))
    kept, unused = y_adjoint(at, returned, jobs[True] + jobs[False], everyone[:1], adds, sums)
    mates = [swap(kept[job][0], "slab", 1) for job in jobs[True]]
    own = [kept[job][0] for job in jobs[False]]
    edges = call(edges_kernel, [(4, rows, depth)] * 2, [place], fields, [], cells, "edges", first=sums[:1])
    halos = (swap(edges[0], "slab", 1), swap_outward(edges[1], "slab"), *[one[0] for one in others])
    (lapped,) = call(
        functools.partial(laplace_kernel, refls),
        [(4, planes, rows, depth)],
        [place],
        (*fields, *halos),
        [],
        30 * cells,
        "laplace",
    )
    result = ()
    for part in range(splits):
        result = call(
            functools.partial(final_kernel, refls),
            [(planes, rows, depth), (3, planes, rows, depth)],
            [place, *params],
            (
                amplitude,
                support,
                lapped,
                own[part],
                mates[part],
                *[one[part] for one in others],
                *[made[part][k][0] for k in range(refls)],
            ),
            [],
            20 * refls * cells // splits,
            "final",
            {
                0: ((portion, rows, depth), (part, 0, 0)),
                1: ((portion, rows * refls, depth), (part, 0, 0)),
                2: ((4, portion, rows, depth), (0, part, 0, 0)),
            },
            out_blocks=[((portion, rows, depth), (part, 0, 0)), ((3, portion, rows, depth), (0, part, 0, 0))],
            carried=result,
        )
    return tuple(result)


def solution(mesh):
    placed = (
        P("slab", "refl", None),
        P(None, "slab", "refl", None),
        P("slab", None, None),
        P("refl", None),
        P("refl"),
        P("refl", None, "slab", None),
    )
    return jax.shard_map(
        body,
        mesh=mesh,
        in_specs=placed,
        out_specs=(P("slab", "refl", None), P(None, "slab", "refl", None)),
        check_vma=False,
    )
```

```python
import functools

import jax
import jax.numpy as jnp
import ml_dtypes
import numpy as np
from jax import lax
from jax.experimental import pallas as pl
from jax.experimental.pallas import tpu as pltpu
from jax.sharding import PartitionSpec as P

STRAIN_WEIGHT = 0.05
EDGE_WEIGHT = 0.05
PIECES = (8, 8)
F32 = jnp.float32
BF16 = jnp.bfloat16


def split_table(table):
    high = table.astype(ml_dtypes.bfloat16)
    low = (table - high.astype(np.float64)).astype(ml_dtypes.bfloat16)
    return high, low


def forward_table(freqs, places, length):
    angle = 2.0 * np.pi / length * (freqs[:, None] * places[None, :] % length)
    cosine = np.cos(angle) * length ** (-0.5)
    sine = np.sin(angle) * length ** (-0.5)
    return np.block([[cosine, sine], [-sine, cosine]])


def turn_fits():
    nodes = np.cos(np.pi * (np.arange(400) + 0.5) / 400)
    t = (nodes + 1.0) / 8.0
    r = np.sqrt(t)
    fits = []
    for values, degree in ((np.cos(2 * np.pi * r), 8), (np.sin(2 * np.pi * r) / r, 8)):
        cheb = np.polynomial.chebyshev.Chebyshev.fit(t, values, degree, domain=[0.0, 0.25])
        fits.append([float(c) for c in cheb.convert(kind=np.polynomial.Polynomial).coef])
    return fits


COS_FIT, SIN_FIT = turn_fits()


def series(coefs, t):
    total = jnp.full_like(t, coefs[-1])
    for coef in coefs[-2::-1]:
        total = total * t + coef
    return total


def halves(x):
    high = x.astype(BF16)
    return high, (x - high.astype(F32)).astype(BF16)


def dot(a, b):
    return jnp.dot(a, b, preferred_element_type=F32)


def dot_pairs(a, b):
    return dot(a[0], b[0]) + (dot(a[0], b[1]) + dot(a[1], b[0]))


SMEM = pl.BlockSpec(memory_space=pltpu.SMEM)


def whole(shape):
    return pl.BlockSpec(tuple(shape), lambda step, rank=len(shape): (0,) * rank)


def call(kernel, outs, scalars, operands, scratch, flops, name, blocks=None, first=(), vmem=48, out_blocks=None, carried=()):
    blocks = blocks or {}
    inputs = len(scalars) + len(operands)
    specs = [SMEM] * len(scalars)
    moved = 4 * sum(int(np.prod(shape)) for shape in outs)
    for at, operand in enumerate(operands):
        if at in blocks and blocks[at] is None:
            shape = (0,)
            specs.append(pl.BlockSpec(memory_space=pl.ANY))
        elif at in blocks:
            shape, index = blocks[at]
            specs.append(pl.BlockSpec(shape, lambda step, index=index: index))
        else:
            shape = operand.shape
            specs.append(whole(shape))
        moved += int(np.prod(shape)) * operand.dtype.itemsize
    first = (*first, *carried)
    specs += [pl.BlockSpec(memory_space=pl.ANY)] * len(first)
    aliases = {len(specs) - len(carried) + i: i for i in range(len(carried))}

    def run(*refs):
        kernel(*refs[:inputs], *refs[inputs + len(first) :])

    return pl.pallas_call(
        run,
        grid=(1,),
        out_shape=[jax.ShapeDtypeStruct(shape, F32) for shape in outs],
        in_specs=specs,
        out_specs=[
            pl.BlockSpec(shape, lambda step, index=index: index)
            for shape, index in out_blocks or [(shape, (0,) * len(shape)) for shape in outs]
        ],
        input_output_aliases=aliases,
        scratch_shapes=scratch,
        compiler_params=pltpu.CompilerParams(vmem_limit_bytes=vmem * 1024 * 1024),
        cost_estimate=pl.CostEstimate(flops=int(flops), bytes_accessed=int(moved), transcendentals=0),
        name=name,
    )(*scalars, *operands, *first)


def field_of(place, amp, disp, sup, f, p):
    if f > 0:
        return disp[f - 1, p]
    rows = amp.shape[1]
    return sup[p, pl.ds(pl.multiple_of(place[2] * rows, rows), rows), :].astype(F32) * amp[p]


def edges_kernel(place, amp, disp, sup, x_mate, x_out):
    planes = amp.shape[0]
    core = place[1]
    for f in range(4):
        x_mate[f] = field_of(place, amp, disp, sup, f, (1 - core) * (planes - 1))
        x_out[f] = field_of(place, amp, disp, sup, f, core * (planes - 1))


def pack_kernel(edged, place, a, b, amp, disp, sup, out):
    portion, rows, depth = a.shape[1:]
    planes = amp.shape[0]
    for c in range(2):
        for p in range(portion):
            at = (c * portion + p) * rows
            out[at : at + rows, :] = a[c, p] + b[c, p]
    if edged:
        for f in range(4):
            for p in range(planes):
                value = field_of(place, amp, disp, sup, f, p)
                at = 2 * portion * rows + f * planes + p
                out[at : at + 1, :] = value[:1]
                at += 4 * planes
                out[at : at + 1, :] = value[rows - 1 :]


def laplace_kernel(refls, place, amp, disp, sup, x_mate, x_out, *refs):
    planes, rows, depth = amp.shape
    packs, out = refs[:-1], refs[-1]
    refl = place[2]
    low_core = place[1] == 0
    row = lax.broadcasted_iota(jnp.int32, (rows, depth), 0)
    lane = lax.broadcasted_iota(jnp.int32, (rows, depth), 1)
    for f in range(4):
        for p in range(planes):
            centre = field_of(place, amp, disp, sup, f, p)
            before, behind = jnp.zeros((1, depth), F32), jnp.zeros((1, depth), F32)
            for k in range(1, refls):
                at = packs[k - 1].shape[0] - 8 * planes + f * planes + p
                behind = jnp.where((refl ^ k) - refl == 1, packs[k - 1][at : at + 1, :], behind)
                at += 4 * planes
                before = jnp.where(refl - (refl ^ k) == 1, packs[k - 1][at : at + 1, :], before)
            if p == 0:
                beside = jnp.where(low_core, x_out[f], x_mate[f])
            else:
                beside = field_of(place, amp, disp, sup, f, p - 1)
            if p == planes - 1:
                beside = beside + jnp.where(low_core, x_mate[f], x_out[f])
            else:
                beside = beside + field_of(place, amp, disp, sup, f, p + 1)
            beside = beside + jnp.where(row == 0, before, pltpu.roll(centre, 1, 0))
            beside = beside + jnp.where(row == rows - 1, behind, pltpu.roll(centre, rows - 1, 0))
            beside = beside + jnp.where(lane == 0, 0.0, pltpu.roll(centre, 1, 1))
            beside = beside + jnp.where(lane == depth - 1, 0.0, pltpu.roll(centre, depth - 1, 1))
            out[f, p] = 6.0 * centre - beside


def object_kernel(which, grid, place, *refs):
    params, (amp, disp, sup), outs = refs[: len(which)], refs[len(which) : len(which) + 3], refs[len(which) + 3 :]
    planes, rows, depth = amp.shape
    first = pl.multiple_of(place[2] * rows, rows)
    zed = lax.broadcasted_iota(jnp.int32, (rows, depth), 1).astype(F32) * (1.0 / grid)

    def plane(p, carry):
        weight = sup[p, pl.ds(first, rows), :].astype(F32) * amp[p]
        parts = [disp[0, p], disp[1, p], disp[2, p]]
        for at, param in enumerate(params):
            phase = param[0] * parts[0] + param[1] * parts[1] + param[2] * parts[2]
            shifted = param[3] * zed
            turns = phase * (0.5 / np.pi) + (shifted - jnp.floor(shifted))
            turns = turns - jnp.floor(turns + 0.5)
            square = turns * turns
            cosine = series(COS_FIT, square)
            sine = series(SIN_FIT, square) * turns
            outs[2 * at][0, p] = cosine
            outs[2 * at][1, p] = sine
            outs[2 * at + 1][0, p] = weight * cosine
            outs[2 * at + 1][1, p] = weight * sine
        return carry

    lax.fori_loop(0, planes, plane, 0)


def y_forward_kernel(refls, chips, splits, targets, place, *refs):
    count = 2 * refls * splits
    parts, tables, outs = refs[:count], refs[count], refs[count + 1 : -2]
    hold_high, hold_low = refs[-2:]
    chip, core, refl = place[0], place[1], place[2]
    portion, rows, depth = parts[0].shape[1:]
    planes = portion * splits
    length = rows * refls
    share = tables.shape[2] // chips

    def order(which):
        return jnp.concatenate(
            [tables[core, which, pl.ds(pl.multiple_of((chip ^ k) * share, share), share), :] for k in targets],
            axis=0,
        )

    table = (order(0), order(1))
    for src in range(2):
        for p in range(planes):
            lane = (src * planes + p) * depth
            for c in range(2):
                for k in range(refls):
                    part = parts[(src * refls + k) * splits + p // portion]
                    one, two = halves(part[c, p % portion])
                    at = pl.ds(pl.multiple_of(c * length + (refl ^ k) * rows, rows), rows)
                    hold_high[at, lane : lane + depth] = one
                    hold_low[at, lane : lane + depth] = two
    for src in range(2):
        for p in range(0, planes, 2):
            lane = (src * planes + p) * depth
            operand = (hold_high[:, lane : lane + 2 * depth], hold_low[:, lane : lane + 2 * depth])
            result = dot_pairs(table, operand)
            base = (core if src == 0 else 1 - core) * planes + p
            for i in range(len(targets)):
                for j in range(2):
                    outs[i][base + j] = result[i * share : (i + 1) * share, j * depth : (j + 1) * depth]


def middle_kernel(chips, first, place, *refs):
    got, intensity = refs[:chips], refs[chips]
    fwd = (refs[chips + 1][...], refs[chips + 2][...])
    bwd = (refs[chips + 3][...], refs[chips + 4][...])
    outs = refs[chips + 5 : -4]
    gather, scatter, measured, arrived = refs[-4:]
    chip = place[0]
    group, width, depth = got[0].shape
    rows = width // 2
    edge = group * chips
    grid = 2 * edge
    batch = gather.shape[1] // depth
    held = first // 8 * 8
    load = pltpu.make_async_copy(intensity.at[0, :, held : held + measured.shape[1], :], measured, arrived)
    load.start()

    def place_of(c, k):
        return pl.ds(pl.multiple_of(c * edge + (chip ^ k) * group, group), group)

    for key in range(0, rows, batch):
        for k in range(chips):
            for c in range(2):
                for j in range(batch):
                    gather[place_of(c, k), j * depth : (j + 1) * depth] = got[k][:, (key + j) * 2 + c, :]
        one = dot_pairs(fwd, halves(gather[...]))
        if key == 0:
            load.wait()
        back = []
        for j in range(batch):
            lines = [one[c * grid : (c + 1) * grid, j * depth : (j + 1) * depth] for c in range(2)]
            spectrum = dot_pairs(halves(jnp.concatenate(lines, axis=1)), bwd)
            real, imag = spectrum[:, :grid], spectrum[:, grid:]
            excess = 4.0 * (real * real + imag * imag - measured[:, first - held + key + j, :])
            back.append(dot_pairs(halves(jnp.concatenate([excess * real, excess * imag], axis=1)), fwd))
        lines = [jnp.concatenate([b[:, c * depth : (c + 1) * depth] for b in back], axis=1) for c in range(2)]
        scatter[...] = dot_pairs(bwd, halves(jnp.concatenate(lines, axis=0)))
        for k in range(chips):
            for c in range(2):
                for j in range(batch):
                    outs[k][:, (key + j) * 2 + c, :] = scatter[place_of(c, k), j * depth : (j + 1) * depth]


def y_adjoint_kernel(chips, jobs, parts, place, *refs):
    got, tables = refs[:chips], refs[chips]
    total = len(parts) * len(jobs)
    adds, outs = refs[chips + 1 : -2 - total], refs[-2 - total : -2]
    done, hold = refs[-2:]
    done[...] = jnp.zeros_like(done)
    chip, core, refl = place[0], place[1], place[2]
    planes, rows, depth = outs[0].shape[1:]
    width = got[0].shape[1]

    def order(which):
        pieces = []
        for q in parts:
            for c in range(2):
                at = pl.multiple_of(((refl ^ q) * 2 + c) * rows, rows)
                pieces.append(tables[core, which, pl.ds(at, rows), :])
        return jnp.concatenate(pieces, axis=0)

    table = (order(0), order(1))
    for job, (mate, first) in enumerate(jobs):
        base = (1 - core if mate else core) * (got[0].shape[0] // 2) + first
        for p in range(planes):
            lane = (job * planes + p) * depth
            for k in range(chips):
                at = pl.ds(pl.multiple_of((chip ^ k) * width, width), width)
                hold[at, lane : lane + depth] = got[k][base + p]
    for job in range(len(jobs)):
        for p in range(0, planes, 2):
            lane = (job * planes + p) * depth
            result = dot_pairs(table, halves(hold[:, lane : lane + 2 * depth]))
            for i in range(len(parts)):
                for c in range(2):
                    at = (i * 2 + c) * rows
                    for j in range(2):
                        value = result[at : at + rows, j * depth : (j + 1) * depth]
                        if adds:
                            value = value + adds[job * len(parts) + i][c, p + j]
                        outs[job * len(parts) + i][c, p + j] = value


def final_kernel(refls, place, *refs):
    params = refs[:refls]
    amp, sup, lapped, own, mate = refs[refls : refls + 5]
    others, phases = refs[refls + 5 : 2 * refls + 4], refs[2 * refls + 4 : -2]
    out_amp, out_disp = refs[-2:]
    planes, rows, depth = amp.shape
    first = pl.multiple_of(place[2] * rows, rows)

    def plane(p, carry):
        mask = sup[p, pl.ds(first, rows), :].astype(F32)
        weight = mask * amp[p]
        total = jnp.zeros((rows, depth), F32)
        moved = [jnp.zeros((rows, depth), F32) for _ in range(3)]
        for k in range(refls):
            if k == 0:
                real, imag = [own[c, p] + mate[c, p] for c in range(2)]
            else:
                at = [pl.ds(pl.multiple_of((c * planes + p) * rows, rows), rows) for c in range(2)]
                real, imag = [others[k - 1][at[c], :] for c in range(2)]
            cosine, sine = phases[k][0, p], phases[k][1, p]
            total = total + (real * cosine + imag * sine)
            across = weight * (imag * cosine - real * sine)
            moved = [m + params[k][c] * across for c, m in enumerate(moved)]
        out_amp[p] = mask * total + (2.0 * EDGE_WEIGHT) * (mask * lapped[0, p])
        for c in range(3):
            out_disp[c, p] = moved[c] + (2.0 * STRAIN_WEIGHT) * lapped[c + 1, p]
        return carry

    lax.fori_loop(0, planes, plane, 0)


def swap(x, axis, bits):
    count = lax.axis_size(axis)
    return lax.ppermute(x, axis, [(i, i ^ bits) for i in range(count)])


def swap_outward(x, axis):
    count = lax.axis_size(axis)
    return lax.ppermute(x, axis, [pair for i in range(1, count - 1, 2) for pair in ((i, i + 1), (i + 1, i))])


def body(amplitude, displacement, support, miller, shift_kz, intensity):
    refls = lax.axis_size("refl")
    slabs = lax.axis_size("slab")
    chips = slabs // 2
    planes, rows, depth = amplitude.shape
    edge = planes * slabs
    grid = 2 * edge
    keys = grid // slabs
    pieces = PIECES if sum(PIECES) == keys else (keys,)
    splits = 2 if planes % 8 == 0 else 1
    portion = planes // splits
    group = 2 * planes
    refl = lax.axis_index("refl")
    slab = lax.axis_index("slab")
    place = jnp.stack([slab // 2, slab % 2, refl]).astype(jnp.int32)
    cells = planes * rows * depth
    part_shape = (2, portion, rows, depth)

    every, inner = np.arange(grid), np.arange(edge)
    table = forward_table(every, inner, grid)
    constants = [jnp.asarray(t) for one in (table, table.T) for t in split_table(one)]
    by_key = table.reshape(2, chips, 2, keys, 2 * edge).transpose(2, 1, 3, 0, 4)

    def y_tables(at):
        first, count = sum(pieces[:at]), pieces[at]
        some = by_key[:, :, first : first + count].reshape(2, chips * count * 2, 2 * edge)
        fwd = jnp.asarray(np.stack(split_table(some), axis=1))
        some = some.reshape(2, chips * count * 2, 2, refls, rows)
        some = some.transpose(0, 3, 2, 4, 1).reshape(2, 2 * edge, chips * count * 2)
        return fwd, jnp.asarray(np.stack(split_table(some), axis=1))

    own_params = jnp.concatenate([miller[0].astype(F32), shift_kz.astype(F32)])
    fields = (amplitude, displacement, support)
    def part_blocks(part, start=0):
        return {
            start: ((portion, rows, depth), (part, 0, 0)),
            start + 1: ((3, portion, rows, depth), (0, part, 0, 0)),
            start + 2: ((portion, rows * refls, depth), (part, 0, 0)),
        }

    def make(part, which, vmem=48, first=()):
        made = call(
            functools.partial(object_kernel, which, grid),
            [part_shape] * (2 * len(which)),
            [place, *[params[k] for k in which]],
            fields,
            [],
            50 * len(which) * cells // splits,
            "object",
            part_blocks(part),
            first,
            vmem,
        )
        return {k: made[2 * i : 2 * i + 2] for i, k in enumerate(which)}

    params = [own_params] + [swap(own_params, "refl", k) for k in range(1, refls)]
    made = [make(0, list(range(1, refls)), 60)]
    made += [make(part, list(range(1, refls)), 60, [made[0][1][1]]) for part in range(1, splits)]
    held = [swap(made[part][k][1], "refl", k) for k in range(1, refls) for part in range(splits)]
    for part in range(splits):
        made[part].update(make(part, [0]))
    own_parts = [made[part][0][1] for part in range(splits)]
    own_mates = [swap(x, "slab", 1) for x in own_parts]
    mates = [swap(x, "slab", 1) for x in held]

    def y_forward(at, targets, first=()):
        made = call(
            functools.partial(y_forward_kernel, refls, chips, splits, targets),
            [(group, 2 * pieces[at], depth)] * len(targets),
            [place],
            (*own_parts, *held, *own_mates, *mates, y_tables(at)[0]),
            [pltpu.VMEM((2 * edge, group * depth), BF16)] * 2,
            6 * group * depth * 2 * edge * len(targets) * pieces[at] * 2,
            "y_forward",
            first=first,
        )
        return dict(zip(targets, made))

    def middle(at, got):
        first, count = sum(pieces[:at]), pieces[at]
        held = -(-(first + count) // 8) * 8 - first // 8 * 8
        return call(
            functools.partial(middle_kernel, chips, first),
            [(group, 2 * count, depth)] * chips,
            [place],
            (*got, intensity, *constants),
            [pltpu.VMEM((2 * edge, (count if count < 8 else count // 2 if count > 8 else 8) * depth), F32)] * 2
            + [pltpu.VMEM((grid, held, grid), F32), pltpu.SemaphoreType.DMA],
            6 * count * (2 * edge * 2 * grid * depth * 2 + grid * 2 * depth * 2 * grid * 2),
            "middle",
            {chips: None},
        )

    def y_adjoint(at, got, jobs, parts, adds=None, first=()):
        count = pieces[at]
        made = call(
            functools.partial(y_adjoint_kernel, chips, jobs, parts),
            [part_shape] * (len(parts) * len(jobs)) + [(8, 128)],
            [place],
            (*got, y_tables(at)[1], *([adds[job][k] for job in jobs for k in parts] if adds else [])),
            [pltpu.VMEM((chips * 2 * count, len(jobs) * portion * depth), F32)],
            6 * len(jobs) * portion * depth * len(parts) * 2 * rows * chips * 2 * count,
            "y_adjoint",
            first=first,
        )
        each = len(parts)
        return {job: dict(zip(parts, made[i * each : (i + 1) * each])) for i, job in enumerate(jobs)}, made[-1]

    def cross(sends):
        return [sends[0]] + [swap(sends[k], "slab", 2 * k) for k in range(1, chips)]

    arrived, first = [], ()
    for at in range(len(pieces)):
        arrived.append(cross(y_forward(at, list(range(chips)), first)))
        first = [arrived[at][chips // 2]]
    jobs = {mate: [(mate, part * portion) for part in range(splits)] for mate in (True, False)}
    everyone = list(range(refls))
    adds = None
    for at in range(len(pieces)):
        backs = middle(at, arrived[at])
        returned = cross(backs)
        if at + 1 < len(pieces):
            adds, unused = y_adjoint(at, returned, jobs[True] + jobs[False], everyone, adds)

    for_mate, done = y_adjoint(at, returned, jobs[True], everyone[1:], adds)
    mine, unused = y_adjoint(at, returned, jobs[False], everyone[1:], adds, (done,))
    sums, others = [], [[] for _ in range(1, refls)]
    for part in range(splits):
        for k in range(1, refls):
            shape = (2 * portion * rows + (8 * planes if part == 0 else 0), depth)
            from_mate = swap(for_mate[jobs[True][part]][k], "slab", 1)
            (total,) = call(
                functools.partial(pack_kernel, part == 0),
                [shape],
                [place],
                (mine[jobs[False][part]][k], from_mate, *fields),
                [],
                4 * cells,
                "pack",
            )
            sums.append(total)
            others[k - 1].append(swap(total, "refl", k))
    for_mate, unused = y_adjoint(at, returned, jobs[True], everyone[:1], adds, sums)
    mine, unused = y_adjoint(at, returned, jobs[False], everyone[:1], adds, sums)
    mates = [swap(for_mate[job][0], "slab", 1) for job in jobs[True]]
    own = [mine[job][0] for job in jobs[False]]
    edges = call(edges_kernel, [(4, rows, depth)] * 2, [place], fields, [], cells, "edges", first=sums[:1])
    halos = (swap(edges[0], "slab", 1), swap_outward(edges[1], "slab"), *[one[0] for one in others])
    (lapped,) = call(
        functools.partial(laplace_kernel, refls),
        [(4, planes, rows, depth)],
        [place],
        (*fields, *halos),
        [],
        30 * cells,
        "laplace",
    )
    result = ()
    for part in range(splits):
        result = call(
            functools.partial(final_kernel, refls),
            [(planes, rows, depth), (3, planes, rows, depth)],
            [place, *params],
            (
                amplitude,
                support,
                lapped,
                own[part],
                mates[part],
                *[one[part] for one in others],
                *[made[part][k][0] for k in range(refls)],
            ),
            [],
            20 * refls * cells // splits,
            "final",
            {
                0: ((portion, rows, depth), (part, 0, 0)),
                1: ((portion, rows * refls, depth), (part, 0, 0)),
                2: ((4, portion, rows, depth), (0, part, 0, 0)),
            },
            out_blocks=[((portion, rows, depth), (part, 0, 0)), ((3, portion, rows, depth), (0, part, 0, 0))],
            carried=result,
        )
    return tuple(result)


def solution(mesh):
    placed = (
        P("slab", "refl", None),
        P(None, "slab", "refl", None),
        P("slab", None, None),
        P("refl", None),
        P("refl"),
        P("refl", None, "slab", None),
    )
    return jax.shard_map(
        body,
        mesh=mesh,
        in_specs=placed,
        out_specs=(P("slab", "refl", None), P(None, "slab", "refl", None)),
        check_vma=False,
    )
```
